32 devices in a mesh: ctx: 8 (over z, y), fsdp: 4 (over x, core).
Axes of the slice: x: 2, y: 2, z: 4, core: 2. Of those that a mesh axis runs over, the one named last changes fastest.
Arguments:
- block_in: bfloat16 [4, 1024, 2304], P('fsdp', 'ctx'), may hold values from -6 to 6
- stretch_order: int32 [8, 2], replicated, may hold values from 0 to 15, as said below
- weight_query: bfloat16 [2304, 2048], P(None, ('fsdp', 'ctx')), may hold values from -0.625 to 0.625
- weight_key: bfloat16 [2304, 1024], P(None, ('fsdp', 'ctx')), may hold values from -0.125 to 0.125
- weight_value: bfloat16 [2304, 1024], P(None, ('fsdp', 'ctx')), may hold values from -0.125 to 0.125
- weight_output: bfloat16 [2048, 2304], P(('fsdp', 'ctx')), may hold values from -0.125 to 0.125
- weight_gate: bfloat16 [2304, 9216], P(None, ('fsdp', 'ctx')), may hold values from -0.125 to 0.125
- weight_up: bfloat16 [2304, 9216], P(None, ('fsdp', 'ctx')), may hold values from -0.125 to 0.125
- weight_down: bfloat16 [9216, 2304], P(('fsdp', 'ctx')), may hold values from -0.0625 to 0.0625
- gain_preattn: float32 [2304], P(('ctx', 'fsdp')), may hold values from 0.1 to 1.9
- gain_postattn: float32 [2304], P(('ctx', 'fsdp')), may hold values from 0.1 to 1.9
- gain_premlp: float32 [2304], P(('ctx', 'fsdp')), may hold values from 0.1 to 1.9
- gain_postmlp: float32 [2304], P(('ctx', 'fsdp')), may hold values from 0.1 to 1.9
- grad_out: bfloat16 [4, 1024, 2304], P('fsdp', 'ctx'), may hold values from -6 to 6
Outputs:
- block_out: bfloat16 [4, 1024, 2304], P('fsdp', 'ctx')
- grad_in: float32 [4, 1024, 2304], P('fsdp', 'ctx')
- grad_query: float32 [2304, 2048], P(None, ('fsdp', 'ctx'))
- grad_key: float32 [2304, 1024], P(None, ('fsdp', 'ctx'))
- grad_value: float32 [2304, 1024], P(None, ('fsdp', 'ctx'))
- grad_output: float32 [2048, 2304], P(('fsdp', 'ctx'))
- grad_gate: float32 [2304, 9216], P(None, ('fsdp', 'ctx'))
- grad_up: float32 [2304, 9216], P(None, ('fsdp', 'ctx'))
- grad_down: float32 [9216, 2304], P(('fsdp', 'ctx'))
- grad_preattn: float32 [2304], P(('ctx', 'fsdp'))
- grad_postattn: float32 [2304], P(('ctx', 'fsdp'))
- grad_premlp: float32 [2304], P(('ctx', 'fsdp'))
- grad_postmlp: float32 [2304], P(('ctx', 'fsdp'))
The draws below stay inside these ranges and needn't reach their ends.
Inputs may be any that keep to these rules, and one draw needn't show every extreme that they name: `stretch_order`: row c holds the stretch numbers p and 15 - p, where p runs over a permutation of 0 to 7.
All inputs are finite; a program needn't handle non-finite values.
Results may differ from the reference program's by a relative error of at most 0.028.
The reference program's roundings to bfloat16 on the way count: a program that leaves them out, or rounds other values in their place, can miss the bound.
Values may be sent and summed in bfloat16 or wider, within the bound.
No kernel may reach another device: no remote copies, remote signals or barrier semaphores. Data moves between devices by JAX's collectives and lax.ppermute only.
A program may use at most 192 MiB of HBM per device.

```python
import math
import jax
import jax.numpy as jnp
from jax import lax

D = 2304
HEADS = 8
KV_HEADS = 4
HEAD_DIM = 256
FF = 9216
TOK_DEV = 128
LENGTH = 1024
SEQS = 4
N_CTX = 8


def draw_stretch_order(key, part):
    key = jax.random.fold_in(key, 11)
    chosen = jax.random.permutation(key, N_CTX).astype(jnp.int32)
    return jnp.stack([chosen, 2 * N_CTX - 1 - chosen], axis=1)


def block_levels(key, dims, shards, low, high):
    def one(dim, shards_of):
        draws = jax.random.uniform(jax.random.fold_in(jax.random.fold_in(key, 6), dim), (shards_of,), jnp.float32, low / len(shards), high / len(shards))
        return jnp.repeat(jnp.exp(draws), dims[dim] // shards_of).reshape((-1,) + (1,) * (len(dims) - dim - 1))

    loudness = one(*shards[0])
    for cut in shards[1:]:
        loudness = loudness * one(*cut)
    return loudness


def noise(stream_key, extent, scale, most, shards=(), kind=jnp.bfloat16):
    level = block_levels(stream_key, extent, shards, -0.22, 0.18) if shards else 1.0
    array = jax.random.normal(stream_key, extent, jnp.float32) * scale * level
    return jnp.minimum(jnp.maximum(array, -most), most).astype(kind)


def setup_inputs(seed: int = 0) -> dict:
    key_list = jax.random.split(jax.random.key(seed), 15)
    return {
        "block_in": noise(key_list[0], (SEQS, LENGTH, D), 1.0, 6.0, ((0, 4), (1, 8))),
        "stretch_order": draw_stretch_order(jax.random.fold_in(key_list[14], 71), 0),
        "weight_query": noise(key_list[2], (D, HEADS * HEAD_DIM), (D // 24) ** -0.5, 0.625, ((1, 32),)),
        "weight_key": noise(key_list[3], (D, KV_HEADS * HEAD_DIM), D ** -0.5, 0.125, ((1, 32),)),
        "weight_value": noise(key_list[4], (D, KV_HEADS * HEAD_DIM), D ** -0.5, 0.125, ((1, 32),)),
        "weight_output": noise(key_list[5], (HEADS * HEAD_DIM, D), (HEADS * HEAD_DIM) ** -0.5, 0.125, ((0, 32),)),
        "weight_gate": noise(key_list[6], (D, FF), D ** -0.5, 0.125, ((1, 32),)),
        "weight_up": noise(key_list[7], (D, FF), D ** -0.5, 0.125, ((1, 32),)),
        "weight_down": noise(key_list[8], (FF, D), FF ** -0.5, 0.0625, ((0, 32),)),
        "gain_preattn": jnp.clip(1.0 + 0.18 * jax.random.normal(key_list[9], (D,), jnp.float32), 0.1, 1.9),
        "gain_postattn": jnp.clip(1.0 + 0.18 * jax.random.normal(key_list[10], (D,), jnp.float32), 0.1, 1.9),
        "gain_premlp": jnp.clip(1.0 + 0.18 * jax.random.normal(key_list[11], (D,), jnp.float32), 0.1, 1.9),
        "gain_postmlp": jnp.clip(1.0 + 0.18 * jax.random.normal(key_list[12], (D,), jnp.float32), 0.1, 1.9),
        "grad_out": noise(key_list[13], (SEQS, LENGTH, D), 1.0, 6.0, ((0, 4), (1, 8))),
    }


EPS = 1e-06
CAP = 50.0
NEGATIVE = -1e+30
HIGH = lax.Precision.HIGHEST

@jax.custom_vjp
def low(v):
    return lax.optimization_barrier(v.astype(jnp.bfloat16)).astype(jnp.float32)

@jax.custom_vjp
def low_back(v):
    return v

def low_keep(v):
    return (low(v), None)

def low_pass(kept, grad):
    return (grad,)

def back_keep(v):
    return (v, None)

def back_low(kept, grad):
    return (low(grad),)
low.defvjp(low_keep, low_pass)
low_back.defvjp(back_keep, back_low)

def rms_norm(values, gain):
    return values * lax.rsqrt(lax.optimization_barrier(jnp.mean(values * values, axis=-1, keepdims=True)) + EPS) * gain

def rotate(values, cosine, sine):
    middle = values.shape[-1] // 2
    first = values[..., :middle]
    second = values[..., middle:]
    return jnp.concatenate([first * cosine - second * sine, second * cosine + first * sine], axis=-1)

def angles(positions, width):
    steps = jnp.arange(width // 2, dtype=jnp.float32)
    inverse = jnp.exp(steps * (-2.0 * math.log(10000.0) / width))
    return positions.astype(jnp.float32)[:, None] * inverse[None, :]

def positions_of(stretch_order):
    half = TOK_DEV // 2
    storage = jnp.arange(LENGTH, dtype=jnp.int32)
    flat = stretch_order.reshape(-1).astype(jnp.int32)
    return flat[storage // half] * half + storage % half

def attend(queries, keys, values, positions):
    group = queries.shape[1] // keys.shape[1]
    keys = jnp.repeat(keys, group, axis=1)
    values = jnp.repeat(values, group, axis=1)
    block = math.gcd(LENGTH, 512)
    query_blocks = queries.reshape(LENGTH // block, block, queries.shape[1], queries.shape[2])
    position_blocks = positions.reshape(LENGTH // block, block)

    def one_block(pair):
        query_block, query_pos = pair
        scores = low_back(jnp.einsum('qhd,khd->hqk', query_block, keys, precision=HIGH))
        capped = CAP * jnp.tanh(scores / CAP)
        allowed = positions[None, None, :] <= query_pos[None, :, None]
        probs = jax.nn.softmax(jnp.where(allowed, capped, NEGATIVE), axis=-1)
        return jnp.einsum('hqk,khd->qhd', low(probs), values, precision=HIGH)
    result = lax.map(jax.checkpoint(one_block), (query_blocks, position_blocks))
    return result.reshape(LENGTH, queries.shape[1], queries.shape[2])

def forward(rows_all, weight_query, weight_key, weight_value, weight_output, weight_gate, weight_up, weight_down, gain_preattn, gain_postattn, gain_premlp, gain_postmlp, positions):
    angle = angles(positions, HEAD_DIM)
    cosine = jnp.cos(angle)[:, None, :]
    sine = jnp.sin(angle)[:, None, :]
    scale = HEAD_DIM ** (-0.5)

    def one_sequence(rows):
        normed_one = low(rms_norm(rows, gain_preattn))
        query_raw = low_back(jnp.dot(normed_one, weight_query, precision=HIGH)).reshape(LENGTH, HEADS, HEAD_DIM)
        key_raw = low_back(jnp.dot(normed_one, weight_key, precision=HIGH)).reshape(LENGTH, KV_HEADS, HEAD_DIM)
        values = low(low_back(jnp.dot(normed_one, weight_value, precision=HIGH))).reshape(LENGTH, KV_HEADS, HEAD_DIM)
        queries = low(rotate(query_raw, cosine, sine) * scale)
        keys = low(rotate(key_raw, cosine, sine))
        mixed = low(low_back(attend(queries, keys, values, positions))).reshape(LENGTH, HEADS * HEAD_DIM)
        attn_out = low_back(jnp.dot(mixed, weight_output, precision=HIGH))
        resid = rows + rms_norm(attn_out, gain_postattn)
        normed_two = low(rms_norm(resid, gain_premlp))
        gate = low_back(jnp.dot(normed_two, weight_gate, precision=HIGH))
        up_proj = low_back(jnp.dot(normed_two, weight_up, precision=HIGH))
        hidden = low(jax.nn.gelu(gate, approximate=True) * up_proj)
        mlp_out = low_back(jnp.dot(hidden, weight_down, precision=HIGH))
        return resid + rms_norm(mlp_out, gain_postmlp)
    return lax.map(jax.checkpoint(one_sequence), rows_all)

def reference(block_in, stretch_order, weight_query, weight_key, weight_value, weight_output, weight_gate, weight_up, weight_down, gain_preattn, gain_postattn, gain_premlp, gain_postmlp, grad_out):
    positions = positions_of(stretch_order)
    floats = [item.astype(jnp.float32) for item in (block_in, weight_query, weight_key, weight_value, weight_output, weight_gate, weight_up, weight_down, gain_preattn, gain_postattn, gain_premlp, gain_postmlp)]

    def apply_block(*items):
        return forward(*items, positions)
    result, pullback = jax.vjp(apply_block, *floats)
    grads = pullback(grad_out.astype(jnp.float32))
    return (result.astype(jnp.bfloat16), grads[0], grads[1], grads[2], grads[3], grads[4], grads[5], grads[6], grads[7], grads[8], grads[9], grads[10], grads[11])
```

```python
import math

import jax
import jax.numpy as jnp
from jax import lax
from jax.sharding import PartitionSpec as P

HEAD_DIM = 256
EPS = 1e-06
CAP = 50.0
NEGATIVE = -1e30
BF16 = jnp.bfloat16
F32 = jnp.float32


def ring_order(size):
    return list(range(0, size, 2)) + list(range(size - 1, 0, -2))


def ring_hop(block, step):
    order = ring_order(lax.axis_size("ctx"))
    size = len(order)
    return lax.ppermute(block, "ctx", [(order[i], order[(i + step) % size]) for i in range(size)])


def ring_member(offset):
    size = lax.axis_size("ctx")
    own = lax.axis_index("ctx")
    place = jnp.where(own % 2 == 0, own // 2, size - 1 - own // 2)
    place = (place + offset) % size
    return jnp.where(place < size // 2, 2 * place, 2 * (size - 1 - place) + 1)


def ring_offsets():
    half = lax.axis_size("ctx") // 2
    offsets = [0]
    for k in range(1, half):
        offsets += [-k, k]
    return offsets + [half]


def ring_gather(own):
    half = lax.axis_size("ctx") // 2
    blocks = [own]
    behind = ahead = own
    for _ in range(1, half):
        behind, ahead = ring_hop(behind, 1), ring_hop(ahead, -1)
        blocks += [behind, ahead]
    middle = own.shape[0] // 2
    far = [ring_hop(behind[:middle], 1), ring_hop(ahead[middle:], -1)]
    return blocks + [jnp.concatenate(far, axis=0)]


def ring_scatter(term):
    half = lax.axis_size("ctx") // 2
    far = term(half).astype(BF16)
    middle = far.shape[0] // 2
    behind, ahead = ring_hop(far[:middle], 1), ring_hop(far[middle:], -1)
    first = True
    for k in range(half - 1, -1, -1):
        if k == 0:
            return term(0) + (behind.astype(F32) + ahead.astype(F32))
        to_ahead, to_behind = term(k), term(-k)
        if first:
            zeros = jnp.zeros_like(behind)
            behind = jnp.concatenate([behind, zeros], axis=0)
            ahead = jnp.concatenate([zeros, ahead], axis=0)
            first = False
        behind = ring_hop((to_ahead + behind.astype(F32)).astype(BF16), 1)
        ahead = ring_hop((to_behind + ahead.astype(F32)).astype(BF16), -1)


def cube_hop(block, mask):
    size = lax.axis_size("fsdp")
    return lax.ppermute(block, "fsdp", [(i, i ^ mask) for i in range(size)])


def cube_gather(own):
    blocks = [own]
    mask = lax.axis_size("fsdp") // 2
    while mask:
        blocks += [cube_hop(block, mask) for block in blocks]
        mask //= 2
    return blocks


def cube_scatter(terms):
    mask = 1
    while len(terms) > 1:
        half = len(terms) // 2
        kept = terms[:half]
        moved = [cube_hop(term.astype(BF16), mask) for term in terms[half:]]
        terms = [a + b.astype(F32) for a, b in zip(kept, moved)]
        mask *= 2
    return terms[0]


def sum_over_all(block):
    for axis in ("fsdp", "ctx"):
        mask = 1
        size = lax.axis_size(axis)
        while mask < size:
            block = block + lax.ppermute(block, axis, [(i, i ^ mask) for i in range(size)])
            mask *= 2
    return block


def rms_norm(values, gain):
    return values * lax.rsqrt(jnp.mean(values * values, axis=-1, keepdims=True) + EPS) * gain


def norm_back(values, gain, cotangent):
    _, pullback = jax.vjp(rms_norm, values, gain)
    return pullback(cotangent)


def rotate(values, cosine, sine):
    middle = values.shape[-1] // 2
    first = values[..., :middle]
    second = values[..., middle:]
    return jnp.concatenate(
        [first * cosine - second * sine, second * cosine + first * sine], axis=-1
    )


def dot(a, b, dims):
    return lax.dot_general(a, b, (dims, ((), ())), preferred_element_type=F32)


def nn(a, b):
    return dot(a, b, ((1,), (0,)))


def nt(a, b):
    return dot(a, b, ((1,), (1,)))


def tn(a, b):
    return dot(a, b, ((0,), (0,)))


def gelu_parts(gate):
    slope = math.sqrt(2.0 / math.pi)
    square = gate * gate
    tanh = jnp.tanh(slope * gate * (1.0 + 0.044715 * square))
    value = 0.5 * gate * (1.0 + tanh)
    inner = slope * (1.0 + 3.0 * 0.044715 * square)
    return value, 0.5 * (1.0 + tanh) + 0.5 * gate * (1.0 - tanh * tanh) * inner


def put_blocks(blocks, places):
    size = blocks[0].shape[0]
    whole = jnp.zeros((size * len(blocks),) + blocks[0].shape[1:], blocks[0].dtype)
    for block, at in zip(blocks, places):
        whole = lax.dynamic_update_slice_in_dim(whole, block, at * size, axis=0)
    return whole


def body(
    block_in,
    stretch_order,
    weight_query,
    weight_key,
    weight_value,
    weight_output,
    weight_gate,
    weight_up,
    weight_down,
    gain_preattn,
    gain_postattn,
    gain_premlp,
    gain_postmlp,
    grad_out,
):
    n_ctx, n_fsdp = lax.axis_size("ctx"), lax.axis_size("fsdp")
    own_ctx, own_fsdp = lax.axis_index("ctx"), lax.axis_index("fsdp")
    rows_in = block_in[0].astype(F32)
    tokens, width = rows_in.shape
    half = tokens // 2
    scale = HEAD_DIM ** (-0.5)
    offsets = ring_offsets()
    members = [ring_member(k) for k in offsets]

    steps = jnp.arange(HEAD_DIM // 2, dtype=F32)
    inverse = jnp.exp(steps * (-2.0 * math.log(10000.0) / HEAD_DIM))

    def positions(member):
        starts = lax.dynamic_slice_in_dim(stretch_order, member, 1, axis=0)[0]
        return (starts[:, None] * half + jnp.arange(half, dtype=jnp.int32)[None, :]).reshape(-1)

    query_pos = positions(own_ctx)
    key_pos = jnp.concatenate([positions(member) for member in members])
    angle = query_pos.astype(F32)[:, None] * inverse[None, :]
    cosine, sine = jnp.cos(angle), jnp.sin(angle)

    gains = jnp.stack([gain_preattn, gain_postattn, gain_premlp, gain_postmlp])
    share = gains.shape[1]
    own_place = (own_ctx * n_fsdp + own_fsdp) * share
    gains = sum_over_all(
        lax.dynamic_update_slice_in_dim(jnp.zeros((4, width), F32), gains, own_place, axis=1)
    )
    gain_one, gain_two, gain_three, gain_four = gains[0], gains[1], gains[2], gains[3]

    query_cols, key_cols = weight_query.shape[1], weight_key.shape[1]
    in_blocks = ring_gather(
        jnp.concatenate([weight_query.T, weight_key.T, weight_value.T], axis=0)
    )
    query_full = put_blocks([b[:query_cols] for b in in_blocks], members)
    key_full = put_blocks([b[query_cols : query_cols + key_cols] for b in in_blocks], members)
    value_full = put_blocks([b[query_cols + key_cols :] for b in in_blocks], members)
    output_full = put_blocks(ring_gather(weight_output), members)
    gate_full = jnp.concatenate(cube_gather(weight_gate.T), axis=0)
    up_full = jnp.concatenate(cube_gather(weight_up.T), axis=0)
    down_full = jnp.concatenate(cube_gather(weight_down), axis=0)

    normed_one = jnp.concatenate(cube_gather(rms_norm(rows_in, gain_one).astype(BF16)), axis=0)
    seqs = n_fsdp
    group = query_full.shape[0] // HEAD_DIM

    def by_head(flat, heads):
        return flat.reshape(seqs, tokens, heads, HEAD_DIM).transpose(0, 2, 1, 3)

    def flatten(heads):
        return heads.transpose(0, 2, 1, 3).reshape(seqs * tokens, -1)

    queries = (rotate(by_head(nt(normed_one, query_full), group), cosine, sine) * scale).astype(BF16)
    queries = queries.reshape(seqs, group * tokens, HEAD_DIM)
    keys_own = rotate(nt(normed_one, key_full).reshape(seqs, tokens, HEAD_DIM), cosine, sine)
    values_own = nt(normed_one, value_full).reshape(seqs, tokens, HEAD_DIM)
    own = jnp.stack([keys_own, values_own], axis=1).astype(BF16)
    both = jnp.concatenate(ring_gather(own), axis=2)
    keys, values = both[:, 0], both[:, 1]
    raw = jnp.einsum("sqd,skd->sqk", queries, keys, preferred_element_type=F32)
    capped = CAP * jnp.tanh(raw / CAP)
    allowed = key_pos[None, :] <= jnp.tile(query_pos, group)[:, None]
    masked = jnp.where(allowed, capped, NEGATIVE)
    best = jnp.max(masked, axis=-1, keepdims=True)
    weights = jnp.exp(masked - best)
    total = jnp.sum(weights, axis=-1, keepdims=True)
    weighted = jnp.einsum("sqk,skd->sqd", weights.astype(BF16), values, preferred_element_type=F32)
    attn_exact = weighted / total
    mixed = flatten(attn_exact.astype(BF16).reshape(seqs, group, tokens, HEAD_DIM))

    def by_seq(flat):
        return [flat[i * tokens : (i + 1) * tokens] for i in range(seqs)]

    attn_out = cube_scatter(by_seq(nn(mixed, output_full)))
    resid = rows_in + rms_norm(attn_out, gain_two)

    normed_two = ring_gather(rms_norm(resid, gain_three).astype(BF16))
    gates = [nt(rows, gate_full) for rows in normed_two]
    ups = [nt(rows, up_full) for rows in normed_two]
    parts = [gelu_parts(gate) for gate in gates]
    hidden = [(part[0] * up).astype(BF16) for part, up in zip(parts, ups)]
    at = {offset: i for i, offset in enumerate(offsets)}
    mlp_out = ring_scatter(lambda k: nn(hidden[at[k]], down_full))
    block_out = resid + rms_norm(mlp_out, gain_four)

    cotangent = grad_out[0].astype(F32)
    d_mlp_out, grad_four = norm_back(mlp_out, gain_four, cotangent)
    d_mlp = ring_gather(d_mlp_out.astype(BF16))
    d_hidden = [nt(rows, down_full) for rows in d_mlp]
    d_gate = [(d * up * part[1]).astype(BF16) for d, up, part in zip(d_hidden, ups, parts)]
    d_up = [(d * part[0]).astype(BF16) for d, part in zip(d_hidden, parts)]
    d_normed_two = ring_scatter(
        lambda k: nn(d_gate[at[k]], gate_full) + nn(d_up[at[k]], up_full)
    )
    d_resid_mlp, grad_three = norm_back(resid, gain_three, d_normed_two)
    d_resid = cotangent + d_resid_mlp
    d_attn_out, grad_two = norm_back(attn_out, gain_two, d_resid)

    normed_two_all = jnp.concatenate(normed_two, axis=0)
    d_mlp_all = jnp.concatenate(d_mlp, axis=0)
    grad_down_full = tn(jnp.concatenate(hidden, axis=0), d_mlp_all)
    grad_gate_full = tn(jnp.concatenate(d_gate, axis=0), normed_two_all)
    grad_up_full = tn(jnp.concatenate(d_up, axis=0), normed_two_all)

    def to_owners(full):
        size = full.shape[0] // n_fsdp
        return cube_scatter([full[i * size : (i + 1) * size] for i in range(n_fsdp)])

    grad_down = to_owners(grad_down_full)
    grad_gate = to_owners(grad_gate_full).T
    grad_up = to_owners(grad_up_full).T

    d_attn = jnp.concatenate(cube_gather(d_attn_out.astype(BF16)), axis=0)
    grad_output_full = tn(mixed, d_attn)
    d_mixed = by_head(nt(d_attn, output_full).astype(BF16), group)
    d_mixed = d_mixed.reshape(seqs, group * tokens, HEAD_DIM)
    delta = jnp.sum(d_mixed.astype(F32) * attn_exact, axis=-1, keepdims=True)
    probs = weights * (1.0 / total)
    d_values = jnp.einsum("sqk,sqd->skd", probs.astype(BF16), d_mixed, preferred_element_type=F32)
    d_probs = jnp.einsum("sqd,skd->sqk", d_mixed, values, preferred_element_type=F32)
    d_scores = (probs * (d_probs - delta) * (1.0 - (capped * (1.0 / CAP)) ** 2)).astype(BF16)
    d_queries = jnp.einsum("sqk,skd->sqd", d_scores, keys, preferred_element_type=F32)
    d_keys = jnp.einsum("sqk,sqd->skd", d_scores, queries, preferred_element_type=F32)
    d_both = jnp.stack([d_keys, d_values], axis=1)

    def both_term(k):
        return lax.slice_in_dim(d_both, at[k] * tokens, (at[k] + 1) * tokens, axis=2)

    d_both_own = ring_scatter(both_term)
    d_query_raw = rotate(
        d_queries.reshape(seqs, group, tokens, HEAD_DIM) * scale, cosine, -sine
    ).astype(BF16)
    d_query_raw = flatten(d_query_raw)
    d_key_raw = rotate(d_both_own[:, 0], cosine, -sine).astype(BF16).reshape(-1, HEAD_DIM)
    d_value_raw = d_both_own[:, 1].astype(BF16).reshape(-1, HEAD_DIM)
    d_normed_one = cube_scatter(
        by_seq(
            nn(d_query_raw, query_full) + nn(d_key_raw, key_full) + nn(d_value_raw, value_full)
        )
    )
    d_rows_attn, grad_one = norm_back(rows_in, gain_one, d_normed_one)
    grad_in = d_resid + d_rows_attn

    def cut(full, k):
        size = full.shape[0] // n_ctx
        return lax.dynamic_slice_in_dim(full, members[at[k]] * size, size, axis=0)

    grad_query_full = tn(d_query_raw, normed_one)
    grad_key_full = tn(d_key_raw, normed_one)
    grad_value_full = tn(d_value_raw, normed_one)
    grad_output = ring_scatter(lambda k: cut(grad_output_full, k))
    grad_ins = ring_scatter(
        lambda k: jnp.concatenate(
            [cut(grad_query_full, k), cut(grad_key_full, k), cut(grad_value_full, k)], axis=0
        )
    )
    grad_query = grad_ins[:query_cols].T
    grad_key = grad_ins[query_cols : query_cols + key_cols].T
    grad_value = grad_ins[query_cols + key_cols :].T

    grad_gains = sum_over_all(jnp.stack([grad_one, grad_two, grad_three, grad_four]))
    grad_gains = lax.dynamic_slice_in_dim(grad_gains, own_place, share, axis=1)
    return (
        block_out[None].astype(BF16),
        grad_in[None],
        grad_query,
        grad_key,
        grad_value,
        grad_output,
        grad_gate,
        grad_up,
        grad_down,
        grad_gains[0],
        grad_gains[1],
        grad_gains[2],
        grad_gains[3],
    )


def solution(mesh):
    rows = P("fsdp", "ctx", None)
    columns = P(None, ("fsdp", "ctx"))
    units = P(("fsdp", "ctx"), None)
    gain = P(("ctx", "fsdp"))
    weights = (columns, columns, columns, units, columns, columns, units)
    return jax.shard_map(
        body,
        mesh=mesh,
        in_specs=(rows, P()) + weights + (gain,) * 4 + (rows,),
        out_specs=(rows, rows) + weights + (gain,) * 4,
        check_vma=False,
    )
```

```python
import functools
import math

import jax
import jax.numpy as jnp
from jax import lax
from jax.experimental import pallas as pl
from jax.experimental.pallas import tpu as pltpu
from jax.sharding import PartitionSpec as P

HEAD_DIM = 256
EPS = 1e-06
CAP = 50.0
NEGATIVE = -1e30
BF16 = jnp.bfloat16
F32 = jnp.float32


def ring_order(size):
    return list(range(0, size, 2)) + list(range(size - 1, 0, -2))


def ring_hop(block, step):
    order = ring_order(lax.axis_size("ctx"))
    size = len(order)
    return lax.ppermute(block, "ctx", [(order[i], order[(i + step) % size]) for i in range(size)])


def ring_member(offset):
    size = lax.axis_size("ctx")
    own = lax.axis_index("ctx")
    place = jnp.where(own % 2 == 0, own // 2, size - 1 - own // 2)
    place = (place + offset) % size
    return jnp.where(place < size // 2, 2 * place, 2 * (size - 1 - place) + 1)


def ring_groups():
    half = lax.axis_size("ctx") // 2
    return [[0]] + [[-k, k] for k in range(1, half)] + [[half]]


def tie(*values):
    return lax.optimization_barrier(values)


def ring_gather(own, use, side=None, state=(), first=()):
    half = lax.axis_size("ctx") // 2
    middle = own.shape[0] // 2
    own, state, result = tie(own, state, first)
    blocks, results = [own], []
    behind = ahead = own
    for i in range(half):
        last = i == half - 1
        if last:
            moved = [ring_hop(behind[:middle], 1), ring_hop(ahead[middle:], -1)]
        else:
            moved = [ring_hop(behind, 1), ring_hop(ahead, -1)]
        result = use(i, blocks, result)
        if side:
            state = side(i, state)
        moved, result, state = tie(moved, result, state)
        results.append(result)
        if not last:
            blocks = behind, ahead = moved
    results.append(use(half, moved, result))
    return (results, state) if side else results


def add_terms(terms, moved):
    to_behind, to_ahead = terms
    behind, ahead = (block.astype(F32) for block in moved)
    if behind.shape != to_ahead.shape:
        gap = jnp.zeros_like(behind)
        behind = jnp.concatenate([behind, gap], axis=0)
        ahead = jnp.concatenate([gap, ahead], axis=0)
    return [
        (to_ahead.astype(F32) + behind).astype(BF16),
        (to_behind.astype(F32) + ahead).astype(BF16),
    ]


def ring_scatter(term, operands, side=None, state=(), join=add_terms):
    half = lax.axis_size("ctx") // 2
    far = term(half, operands[half])
    if len(far) == 1:
        middle = far[0].shape[0] // 2
        far = [far[0][:middle], far[0][middle:]]
    sums = [part.astype(BF16) for part in far]
    for i in range(half - 1, -1, -1):
        sums, operand, state = tie(sums, operands[i], state)
        moved = [ring_hop(sums[0], 1), ring_hop(sums[1], -1)]
        terms = term(i, operand)
        if side:
            state = side(i, state)
        moved, terms, state = tie(moved, terms, state)
        if i > 0:
            sums = join(terms, moved)
    return (terms[0], *moved), state


def far_hop(block):
    size = lax.axis_size("fsdp")
    return lax.ppermute(block, "fsdp", [(i, i ^ (size // 2)) for i in range(size)])


def near_hop(block):
    size = lax.axis_size("fsdp")
    return lax.ppermute(block, "fsdp", [(i, i ^ 1) for i in range(size)])


def add_from(block, axis, masks):
    size = lax.axis_size(axis)
    routes = [[(i, i ^ mask) for i in range(size)] for mask in masks if mask < size]
    return sum((lax.ppermute(block, axis, route) for route in routes), block)


def low_masks():
    return range(1, 4)


def high_masks():
    return range(4, lax.axis_size("ctx"), 4)


def rms_norm(values, gain):
    return values * lax.rsqrt(jnp.mean(values * values, axis=-1, keepdims=True) + EPS) * gain


def norm_back(values, gain, cotangent):
    scale = lax.rsqrt(jnp.mean(values * values, axis=-1, keepdims=True) + EPS)
    normal = values * scale
    turned = cotangent * gain
    along = jnp.mean(turned * normal, axis=-1, keepdims=True)
    return scale * (turned - normal * along), jnp.sum(cotangent * normal, axis=0)


def rotate(values, cosine, sine):
    middle = values.shape[-1] // 2
    first = values[..., :middle]
    second = values[..., middle:]
    return jnp.concatenate(
        [first * cosine - second * sine, second * cosine + first * sine], axis=-1
    )


def dot(a, b, dims):
    return lax.dot_general(a, b, (dims, ((), ())), preferred_element_type=F32)


def nn(a, b):
    return dot(a, b, ((1,), (0,)))


def nt(a, b):
    return dot(a, b, ((1,), (1,)))


def tn(a, b):
    return dot(a, b, ((0,), (0,)))


def gelu_parts(gate):
    slope = math.sqrt(2.0 / math.pi)
    square = gate * gate
    tanh = jnp.tanh(slope * gate * (1.0 + 0.044715 * square))
    value = 0.5 * gate * (1.0 + tanh)
    inner = slope * (1.0 + 3.0 * 0.044715 * square)
    return value, 0.5 * (1.0 + tanh) + 0.5 * gate * (1.0 - tanh * tanh) * inner


def normed(values):
    scale = lax.rsqrt(jnp.mean(values * values, axis=-1, keepdims=True) + EPS)
    return values * scale, scale


def pulled(values, gain, cotangent):
    normal, scale = normed(values)
    through = cotangent * gain
    along = jnp.mean(through * normal, axis=-1, keepdims=True)
    return scale * (through - normal * along), jnp.sum(cotangent * normal, axis=0, keepdims=True)


def middle_kernel(rows_ref, kept_ref, moved_ref, gain_two_ref, gain_three_ref, *outs):
    attn_out_ref, resid_ref, normed_two_ref = outs
    attn_out = kept_ref[...] + moved_ref[...].astype(F32)
    resid = rows_ref[...].astype(F32) + normed(attn_out)[0] * gain_two_ref[...]
    attn_out_ref[...] = attn_out
    resid_ref[...] = resid
    normed_two_ref[...] = (normed(resid)[0] * gain_three_ref[...]).astype(BF16)


def end_kernel(term_ref, behind_ref, ahead_ref, resid_ref, grad_ref, gain_ref, *outs):
    block_out_ref, d_mlp_ref, grad_gain_ref = outs
    mlp_out = term_ref[...] + (behind_ref[...].astype(F32) + ahead_ref[...].astype(F32))
    block_out_ref[...] = (resid_ref[...] + normed(mlp_out)[0] * gain_ref[...]).astype(BF16)
    d_mlp, grad_gain_ref[...] = pulled(mlp_out, gain_ref[...], grad_ref[...].astype(F32))
    d_mlp_ref[...] = d_mlp.astype(BF16)


def back_kernel(
    term_ref,
    behind_ref,
    ahead_ref,
    resid_ref,
    attn_out_ref,
    grad_ref,
    gain_two_ref,
    gain_three_ref,
    d_resid_ref,
    d_attn_ref,
    grad_two_ref,
    grad_three_ref,
):
    d_normed = term_ref[...] + (behind_ref[...].astype(F32) + ahead_ref[...].astype(F32))
    d_rows, grad_three_ref[...] = pulled(resid_ref[...], gain_three_ref[...], d_normed)
    d_resid = grad_ref[...].astype(F32) + d_rows
    d_resid_ref[...] = d_resid
    d_attn, grad_two_ref[...] = pulled(attn_out_ref[...], gain_two_ref[...], d_resid)
    d_attn_ref[...] = d_attn.astype(BF16)


def by_rows_call(kernel, args, outs):
    return pl.pallas_call(
        kernel,
        out_shape=[jax.ShapeDtypeStruct(*out) for out in outs],
        compiler_params=pltpu.CompilerParams(vmem_limit_bytes=24 << 20),
        cost_estimate=FREE,
    )(*args)


def input_kernel(seqs, refs_in, refs_w, rows_ref, scale_ref, kept_ref, sent_ref, gain_ref):
    total = sum(nn(d[...], w[...]) for d, w in zip(refs_in, refs_w))
    half = total.shape[0] // 2
    kept_ref[...] = total[:half]
    sent_ref[...] = total[half:].astype(BF16)
    normal = rows_ref[...].astype(F32) * scale_ref[...]
    gain_ref[...] = jnp.sum(total * normal, axis=0, keepdims=True)


def input_terms(ds, weights, rows, scale):
    count, width = rows.shape
    half = count // 2
    tile = tile_of(width, 768)

    def kernel(*refs):
        input_kernel(0, refs[:3], refs[3:6], *refs[6:])

    by_cols = lambda i: (0, i)
    return pl.pallas_call(
        kernel,
        grid=(width // tile,),
        out_shape=[
            jax.ShapeDtypeStruct((half, width), F32),
            jax.ShapeDtypeStruct((half, width), BF16),
            jax.ShapeDtypeStruct((1, width), F32),
        ],
        in_specs=[pl.BlockSpec(d.shape, lambda i: (0, 0)) for d in ds]
        + [pl.BlockSpec((w.shape[0], tile), by_cols) for w in weights]
        + [pl.BlockSpec((count, tile), by_cols), pl.BlockSpec((count, 1), lambda i: (0, 0))],
        out_specs=[
            pl.BlockSpec((half, tile), by_cols),
            pl.BlockSpec((half, tile), by_cols),
            pl.BlockSpec((1, tile), by_cols),
        ],
        compiler_params=ROOMY,
        cost_estimate=FREE,
    )(*ds, *weights, rows, scale)


def stacked(flat):
    heads = flat.shape[1] // HEAD_DIM
    return jnp.concatenate(
        [flat[:, h * HEAD_DIM : (h + 1) * HEAD_DIM] for h in range(heads)], axis=0
    )


def side_by_side(tall, rows):
    return jnp.concatenate(
        [tall[i : i + rows] for i in range(0, tall.shape[0], rows)], axis=1
    )


FREE = pl.CostEstimate(flops=0, bytes_accessed=0, transcendentals=0)
ROOMY = pltpu.CompilerParams(vmem_limit_bytes=56 << 20)


def blank(shapes):
    return pl.pallas_call(
        lambda *refs: None,
        out_shape=[jax.ShapeDtypeStruct(shape, BF16) for shape in shapes],
        out_specs=[pl.BlockSpec(memory_space=pl.ANY)] * len(shapes),
    )()


def place_kernel(cols, n_blocks, members_ref, *refs):
    blocks, outs = refs[:n_blocks], refs[n_blocks + len(cols) :]

    for n, block in enumerate(blocks):

        @pl.when(pl.program_id(0) == n)
        def _(block=block):
            start = 0
            for out, count in zip(outs, cols):
                out[...] = block[start : start + count]
                start += count


def place_rows(fulls, blocks, members, cols):
    width = blocks[0].shape[1]
    if any(count % 16 for count in cols):
        for block, member in zip(blocks, members):
            start = 0
            for m, count in enumerate(cols):
                part = block[start : start + count]
                fulls[m] = lax.dynamic_update_slice_in_dim(fulls[m], part, member * count, axis=0)
                start += count
        return fulls
    n_blocks = len(blocks)
    return pl.pallas_call(
        functools.partial(place_kernel, cols, n_blocks),
        grid_spec=pltpu.PrefetchScalarGridSpec(
            num_scalar_prefetch=1,
            grid=(n_blocks,),
            in_specs=[pl.BlockSpec(block.shape, lambda i, m: (0, 0)) for block in blocks]
            + [pl.BlockSpec(memory_space=pl.ANY)] * len(fulls),
            out_specs=[pl.BlockSpec((count, width), lambda i, m: (m[i], 0)) for count in cols],
        ),
        out_shape=[jax.ShapeDtypeStruct(full.shape, full.dtype) for full in fulls],
        input_output_aliases={1 + n_blocks + m: m for m in range(len(fulls))},
        cost_estimate=FREE,
    )(jnp.stack(members), *blocks, *fulls)


def put_kernel(n_blocks, *refs):
    for n in range(n_blocks):

        @pl.when(pl.program_id(0) == n)
        def _(n=n):
            refs[-1][...] = refs[n][...]


def put_blocks(full, blocks, at, along):
    shape = blocks[0].shape
    where = (lambda i: (i, at, 0)) if along == 0 else (lambda i: (0, at + i, 0))
    return pl.pallas_call(
        functools.partial(put_kernel, len(blocks)),
        grid=(len(blocks),),
        out_shape=jax.ShapeDtypeStruct(full.shape, full.dtype),
        in_specs=[pl.BlockSpec(shape, lambda i: (0, 0, 0))] * len(blocks)
        + [pl.BlockSpec(memory_space=pl.ANY)],
        out_specs=pl.BlockSpec(shape, where),
        input_output_aliases={len(blocks): 0},
        cost_estimate=FREE,
    )(*blocks, full)


def tile_of(count, tile):
    return tile if count % tile == 0 else count


def stack_rows(refs):
    return jnp.concatenate([ref[...] for ref in refs], axis=0) if len(refs) > 1 else refs[0][...]


def weight_grad_kernel(groups, blocks, *refs):
    units, rows, out_ref, all_rows = refs[:groups], refs[groups : groups + blocks], refs[-2], refs[-1]

    @pl.when(pl.program_id(0) == 0)
    def _():
        at = 0
        for row in rows:
            all_rows[at : at + row.shape[0]] = row[...]
            at += row.shape[0]

    out_ref[...] = tn(stack_rows(units), all_rows[...]).astype(BF16)


def weight_grad(units, rows, part=None):
    count, width = units[0].shape[1], rows[0].shape[1]
    total = sum(row.shape[0] for row in rows)
    tile = tile_of(count, 384)
    first, tiles, before = part or (0, count // tile, None)
    first, tiles = min(first, count // tile - 1), min(tiles, count // tile)
    held = [] if before is None else [before]
    return pl.pallas_call(
        functools.partial(weight_grad_kernel, len(units), len(rows)),
        grid=(tiles,),
        out_shape=jax.ShapeDtypeStruct((count, width), BF16),
        in_specs=[pl.BlockSpec((unit.shape[0], tile), lambda i: (0, first + i)) for unit in units]
        + [pl.BlockSpec(row.shape, lambda i: (0, 0)) for row in rows]
        + [pl.BlockSpec(memory_space=pl.ANY)] * len(held),
        out_specs=pl.BlockSpec((tile, width), lambda i: (first + i, 0)),
        scratch_shapes=[pltpu.VMEM((total, width), BF16)],
        input_output_aliases={len(units) + len(rows): 0} if held else {},
        compiler_params=ROOMY,
        cost_estimate=FREE,
    )(*units, *rows, *held)


def expand_kernel(blocks, *refs):
    rows = stack_rows(refs[:blocks])
    gate_ref, up_ref, value_ref, slope_ref, hidden_ref = refs[blocks:]
    gate, up = nt(rows, gate_ref[0]), nt(rows, up_ref[0])
    value, slope = gelu_parts(gate)
    value_ref[...] = value
    slope_ref[...] = up * slope
    hidden_ref[...] = (value * up).astype(BF16)


def contract_kernel(blocks, *refs):
    rows = stack_rows(refs[:blocks])
    down_ref, value_ref, slope_ref, d_gate_ref, d_up_ref = refs[blocks:]
    d_hidden = nt(rows, down_ref[...])
    d_gate_ref[...] = (d_hidden * slope_ref[...]).astype(BF16)
    d_up_ref[...] = (d_hidden * value_ref[...]).astype(BF16)


def unit_call(kernel, rows, weights, units, outs):
    count, width = weights[0][0].shape[-2:]
    total = sum(row.shape[0] for row in rows)
    tile = tile_of(count, 384)
    weight_specs = [
        pl.BlockSpec((1,) * len(at) + (tile, width), lambda i, at=at: (*at, i, 0))
        for _, at in weights
    ]
    flat = pl.BlockSpec((total, tile), lambda i: (0, i))
    return pl.pallas_call(
        functools.partial(kernel, len(rows)),
        grid=(count // tile,),
        out_shape=[jax.ShapeDtypeStruct((total, count), out) for out in outs],
        in_specs=[pl.BlockSpec(row.shape, lambda i: (0, 0)) for row in rows]
        + weight_specs
        + [flat] * len(units),
        out_specs=[flat] * len(outs),
        compiler_params=pltpu.CompilerParams(vmem_limit_bytes=24 << 20),
        cost_estimate=FREE,
    )(*rows, *(weight for weight, _ in weights), *units)


def out_kernel(*refs):
    ins, weights, out_ref = refs[: len(refs) // 2], refs[len(refs) // 2 : -1], refs[-1]
    total = sum(nn(a[...], w[...].reshape(w.shape[-2:])) for a, w in zip(ins, weights))
    out_ref[...] = total.astype(out_ref.dtype)


def out_call(ins, weights, rows, at, out):
    count, width = weights[0][0].shape[-2:]
    tile = tile_of(width, 768)
    return pl.pallas_call(
        out_kernel,
        grid=(width // tile,),
        out_shape=jax.ShapeDtypeStruct((rows, width), out),
        in_specs=[pl.BlockSpec((rows, count), lambda i: (at, 0))] * len(ins)
        + [
            pl.BlockSpec((1,) * len(lead) + (count, tile), lambda i, lead=lead: (*lead, 0, i))
            for _, lead in weights
        ],
        out_specs=pl.BlockSpec((rows, tile), lambda i: (0, i)),
        compiler_params=pltpu.CompilerParams(vmem_limit_bytes=24 << 20),
        cost_estimate=FREE,
    )(*ins, *(weight for weight, _ in weights))


def gather_kernel(counts, *refs):
    ins, outs = refs[len(counts) : -len(counts)], refs[-len(counts) :]
    for out, cols in zip(outs, counts):
        start = 0
        for count in cols:
            out[start : start + count] = ins[0][...].astype(out.dtype)
            start += count
            ins = ins[1:]


def member_rows(parts, dtype):
    width = parts[0][0][0].shape[1]
    counts = [cols for _, cols, _ in parts]
    if any(count % 16 for cols in counts for count in cols):
        return [
            jnp.concatenate(
                [
                    lax.dynamic_slice_in_dim(full, member * c, c, axis=0)
                    for full, c in zip(arrays, cols)
                ],
                axis=0,
            ).astype(dtype)
            for arrays, cols, member in parts
        ]
    return pl.pallas_call(
        functools.partial(gather_kernel, counts),
        grid_spec=pltpu.PrefetchScalarGridSpec(
            num_scalar_prefetch=len(parts),
            grid=(1,),
            in_specs=[
                pl.BlockSpec((count, width), lambda i, *m, side=side: (m[side][0], 0))
                for side, cols in enumerate(counts)
                for count in cols
            ],
            out_specs=[pl.BlockSpec((sum(cols), width), lambda i, *m: (0, 0)) for cols in counts],
        ),
        out_shape=[jax.ShapeDtypeStruct((sum(cols), width), dtype) for cols in counts],
        compiler_params=ROOMY,
        cost_estimate=FREE,
    )(
        *(member.reshape(1) for _, _, member in parts),
        *(array for arrays, _, _ in parts for array in arrays),
    )


def keys_back_kernel(term_ref, behind_ref, ahead_ref, cosine_ref, sine_ref, rows_ref, *outs):
    d_keys_ref, d_values_ref, grad_keys_ref, grad_values_ref = outs
    total = term_ref[...].astype(F32) + (
        behind_ref[...].astype(F32) + ahead_ref[...].astype(F32)
    )
    d_keys = rotate(total[0], cosine_ref[...], -sine_ref[...]).astype(BF16)
    d_keys = d_keys.reshape(-1, HEAD_DIM)
    d_values = total[1].astype(BF16).reshape(-1, HEAD_DIM)
    d_keys_ref[...] = d_keys
    d_values_ref[...] = d_values
    grad_keys_ref[...] = tn(d_keys, rows_ref[...]).astype(BF16)
    grad_values_ref[...] = tn(d_values, rows_ref[...]).astype(BF16)


def keys_back(parts, cosine, sine, rows):
    count, width = rows.shape
    tile = tile_of(width, 768)
    whole = pl.BlockSpec(parts[0].shape, lambda i: (0, 0, 0, 0))
    flat = pl.BlockSpec((count, HEAD_DIM), lambda i: (0, 0))
    angle = pl.BlockSpec(cosine.shape, lambda i: (0, 0))
    tall = pl.BlockSpec((HEAD_DIM, tile), lambda i: (0, i))
    return pl.pallas_call(
        keys_back_kernel,
        grid=(width // tile,),
        out_shape=[jax.ShapeDtypeStruct((count, HEAD_DIM), BF16)] * 2
        + [jax.ShapeDtypeStruct((HEAD_DIM, width), BF16)] * 2,
        in_specs=[whole] * 3 + [angle] * 2 + [pl.BlockSpec((count, tile), lambda i: (0, i))],
        out_specs=[flat] * 2 + [tall] * 2,
        compiler_params=ROOMY,
        cost_estimate=FREE,
    )(*parts, cosine, sine, rows)


def turned(raw, cosine, sine):
    return jnp.concatenate(
        [
            rotate(raw[:, at : at + HEAD_DIM], cosine, sine)
            for at in range(0, raw.shape[1], HEAD_DIM)
        ],
        axis=1,
    )


def queries_kernel(rows_ref, weight_ref, cosine_ref, sine_ref, out_ref):
    raw = nt(rows_ref[...], weight_ref[...])
    out_ref[...] = (turned(raw, cosine_ref[...], sine_ref[...]) * HEAD_DIM ** (-0.5)).astype(BF16)


def keys_kernel(rows_ref, key_ref, value_ref, cosine_ref, sine_ref, out_ref):
    rows = rows_ref[...]
    out_ref[0, 0] = rotate(nt(rows, key_ref[...]), cosine_ref[...], sine_ref[...]).astype(BF16)
    out_ref[1, 0] = nt(rows, value_ref[...]).astype(BF16)


def project(kernel, rows, weights, cosine, sine, out, out_spec):
    tokens, width = cosine.shape[0], rows.shape[1]

    def whole(array):
        return pl.BlockSpec(array.shape, lambda i: (0, 0))

    return pl.pallas_call(
        kernel,
        grid=(rows.shape[0] // tokens,),
        out_shape=jax.ShapeDtypeStruct(out, BF16),
        in_specs=[pl.BlockSpec((tokens, width), lambda i: (i, 0))]
        + [whole(array) for array in (*weights, cosine, sine)],
        out_specs=out_spec,
        compiler_params=pltpu.CompilerParams(vmem_limit_bytes=16 << 20),
        cost_estimate=FREE,
    )(rows, *weights, cosine, sine)


def attend_kernel(keys_ref, values_ref, queries_ref, query_pos_ref, key_pos_ref, mixed_ref):
    queries = stacked(queries_ref[...])
    tanh = jnp.tanh(nt(queries, keys_ref[0]) * (1.0 / CAP))
    weights = jnp.where(key_pos_ref[...] <= query_pos_ref[...], jnp.exp(CAP * tanh), 0.0)
    total = jnp.sum(weights, axis=1, keepdims=True)
    mixed = nn(weights.astype(BF16), values_ref[0]) / total
    mixed_ref[...] = side_by_side(mixed.astype(BF16), queries_ref.shape[0])


def attend_back_kernel(
    keys_ref,
    values_ref,
    queries_ref,
    d_attn_ref,
    d_attn_next_ref,
    output_ref,
    query_pos_ref,
    key_pos_ref,
    cosine_ref,
    sine_ref,
    *refs,
):
    blocks = key_pos_ref.shape[0] // queries_ref.shape[0]
    d_queries_ref, *d_both_refs = refs[-blocks - 2 :]
    rows = queries_ref.shape[0]
    queries = stacked(queries_ref[...])
    d_attn = jnp.where(pl.program_id(0) == 0, d_attn_ref[...], d_attn_next_ref[...])
    d_mixed = stacked(nt(d_attn, output_ref[...]).astype(BF16))
    keys = keys_ref[0]
    tanh = jnp.tanh(nt(keys, queries) * (1.0 / CAP))
    weights = jnp.where(key_pos_ref[...] <= query_pos_ref[...], jnp.exp(CAP * tanh), 0.0)
    probs = weights * (1.0 / jnp.sum(weights, axis=0, keepdims=True))
    d_values = nn(probs.astype(BF16), d_mixed).astype(BF16)
    for n, out in enumerate(d_both_refs[:-2]):
        out[1, 0] = d_values[n * rows : (n + 1) * rows]
    d_both_refs[-1][0, 0] = d_values[(blocks - 1) * rows :]
    d_probs = nt(values_ref[0], d_mixed)
    delta = jnp.sum(probs * d_probs, axis=0, keepdims=True)
    d_scores = (probs * (d_probs - delta) * (1.0 - tanh * tanh)).astype(BF16)
    d_keys = nn(d_scores, queries).astype(BF16)
    for n, out in enumerate(d_both_refs[:-2]):
        out[0, 0] = d_keys[n * rows : (n + 1) * rows]
    d_both_refs[-2][0, 0] = d_keys[(blocks - 1) * rows :]
    d_queries = tn(d_scores, keys) * HEAD_DIM ** (-0.5)
    d_queries = rotate(d_queries, cosine_ref[...], -sine_ref[...])
    d_queries_ref[...] = side_by_side(d_queries.astype(BF16), rows)


def attention_call(kernel, both, seqs, at, outs, args, specs, out_specs, earlier=()):
    count = both.shape[1]
    total = both.shape[0] // 2
    held = len(args) + 2
    return pl.pallas_call(
        kernel,
        grid=(seqs,),
        out_shape=[jax.ShapeDtypeStruct(*out) for out in outs],
        in_specs=[
            pl.BlockSpec((1, count, HEAD_DIM), lambda i: (at(i), 0, 0)),
            pl.BlockSpec((1, count, HEAD_DIM), lambda i: (at(i) + total, 0, 0)),
        ]
        + specs
        + [pl.BlockSpec(memory_space=pl.ANY)] * len(earlier),
        out_specs=out_specs,
        input_output_aliases={held + n: n for n in range(len(earlier))},
        compiler_params=ROOMY,
        cost_estimate=FREE,
    )(both, both, *args, *earlier)


def body(
    block_in,
    stretch_order,
    weight_query,
    weight_key,
    weight_value,
    weight_output,
    weight_gate,
    weight_up,
    weight_down,
    gain_preattn,
    gain_postattn,
    gain_premlp,
    gain_postmlp,
    grad_out,
):
    n_ctx, n_fsdp = lax.axis_size("ctx"), lax.axis_size("fsdp")
    own_ctx, own_fsdp = lax.axis_index("ctx"), lax.axis_index("fsdp")
    rows_in = block_in[0].astype(F32)
    tokens, width = rows_in.shape
    half = tokens // 2
    half_ring = n_ctx // 2
    groups = ring_groups()
    members = [[ring_member(k) for k in group] for group in groups]

    steps = jnp.arange(HEAD_DIM // 2, dtype=F32)
    inverse = jnp.exp(steps * (-2.0 * math.log(10000.0) / HEAD_DIM))

    def positions(member):
        starts = lax.dynamic_slice_in_dim(stretch_order, member, 1, axis=0)[0]
        return (starts[:, None] * half + jnp.arange(half, dtype=jnp.int32)[None, :]).reshape(-1)

    query_pos = positions(own_ctx)
    key_pos = [jnp.concatenate([positions(m) for m in group]) for group in members]
    angle = query_pos.astype(F32)[:, None] * inverse[None, :]
    cosine, sine = jnp.cos(angle), jnp.sin(angle)

    gains = jnp.stack([gain_preattn, gain_postattn, gain_premlp, gain_postmlp])
    share = gains.shape[1]
    own_place = (own_ctx * n_fsdp + own_fsdp) * share
    gains = lax.dynamic_update_slice_in_dim(jnp.zeros((4, width), F32), gains, own_place, axis=1)

    cols = [weight_query.shape[1], weight_key.shape[1], weight_value.shape[1]]
    cols.append(weight_output.shape[0])
    cuts = [sum(cols[:i]) for i in range(len(cols) + 1)]
    own = jnp.concatenate([weight_query.T, weight_key.T, weight_value.T, weight_output], axis=0)

    def place_blocks(i, blocks, placed):
        if i == half_ring:
            member = [ring_member(i)]
            return [
                part
                for n, block in enumerate(blocks)
                for part in place_rows(placed[2 * n : 2 * n + 2], [block], member, cols[2 * n : 2 * n + 2])
            ]
        ends = [i] if i == 0 else [-i, i]
        return list(place_rows(list(placed), list(blocks), [ring_member(k) for k in ends], cols))

    flying = {}

    def prepare(i, state):
        if i == 0:
            gate_own, up_own = state
            rows = [block_in[0], far_hop(block_in[0]), near_hop(block_in[0])]
            own = jnp.stack([gate_own.T, up_own.T])
            return rows, add_from(gains, "fsdp", low_masks()), own
        if i == 1:
            rows, sums, own = state
            flying["gate_up"] = lax.all_gather(own, "fsdp", axis=1, tiled=True)
            rows = [*rows, near_hop(rows[1])]
            return rows, add_from(sums, "ctx", low_masks())
        if i == 2:
            rows, sums = state
            return jnp.concatenate(rows, axis=0), add_from(sums, "ctx", high_masks())
        if i == half_ring - 1:
            rows, sums = state
            long = rows.astype(F32)
            scales = lax.rsqrt(jnp.mean(long * long, axis=-1, keepdims=True) + EPS)
            return rows, scales, (long * scales * sums[0]).astype(BF16), sums
        return state

    results, (all_rows, scales, normed_one, gains) = ring_gather(
        own,
        place_blocks,
        prepare,
        (weight_gate, weight_up),
        blank([(c * n_ctx, width) for c in cols]),
    )
    query_full, key_full, value_full, output_full = results[-1]
    gain_one, gain_two, gain_three, gain_four = gains[0], gains[1], gains[2], gains[3]

    seqs = n_fsdp
    group = query_full.shape[0] // HEAD_DIM

    by_rows = pl.BlockSpec((tokens, group * HEAD_DIM), lambda i: (i, 0))
    both_own = project(
        keys_kernel,
        normed_one,
        [key_full, value_full],
        cosine,
        sine,
        (2, seqs, tokens, HEAD_DIM),
        pl.BlockSpec((2, 1, tokens, HEAD_DIM), lambda i: (0, i, 0, 0)),
    ).reshape(2 * seqs, tokens, HEAD_DIM)

    def take_keys(i, blocks, both):
        return put_blocks(both, list(blocks), max(2 * i - 1, 0), 0 if i == half_ring else 1)

    def keys_side(i, state):
        if i == 0:
            return project(
                queries_kernel,
                normed_one,
                [query_full],
                cosine,
                sine,
                (seqs * tokens, group * HEAD_DIM),
                by_rows,
            )
        if i == 1:
            return state, flying.pop("gate_up"), weight_down
        if i == 2:
            queries, gate_up, own = state
            flying["down"] = lax.all_gather(own, "fsdp", axis=0, tiled=True)
            return queries, gate_up
        return state

    count = tokens * n_ctx
    results, (queries, gate_up) = ring_gather(
        both_own,
        take_keys,
        keys_side,
        (),
        blank([(2 * seqs, count, HEAD_DIM)])[0],
    )
    both = results[-1]
    rows_pos = jnp.tile(query_pos, group)
    key_pos = jnp.concatenate(key_pos)
    def fixed(*shape):
        return pl.BlockSpec(shape, lambda i: (0, 0))

    (mixed,) = attention_call(
        attend_kernel,
        both,
        seqs,
        lambda i: i,
        [(queries.shape, BF16)],
        [queries, rows_pos[:, None], key_pos[None, :]],
        [by_rows, fixed(group * tokens, 1), fixed(1, count)],
        [by_rows],
    )

    def by_seq(flat):
        return [flat[i * tokens : (i + 1) * tokens] for i in range(seqs)]

    def fold(terms):
        moved = near_hop(jnp.stack([term.astype(BF16) for term in terms[2:]]))
        return terms[0] + moved[0].astype(F32), (terms[1] + moved[1].astype(F32)).astype(BF16)

    kept, sent = fold(by_seq(nn(mixed, output_full)))
    row = (tokens, width)
    gain_rows = [gain[None, :] for gain in (gain_two, gain_three, gain_four)]
    attn_out, resid, normed_two_own = by_rows_call(
        middle_kernel,
        [block_in[0], kept, far_hop(sent), *gain_rows[:2]],
        [(row, F32), (row, F32), (row, BF16)],
    )

    gate_weight, up_weight = (gate_up, (0,)), (gate_up, (1,))

    def expand(i, blocks, last):
        weights = [gate_weight, up_weight]
        return unit_call(expand_kernel, blocks, weights, [], [F32, F32, BF16]), list(blocks)

    def finish_down(i, state):
        return flying.pop("down") if i == 0 else state

    results, down_full = ring_gather(normed_two_own, expand, finish_down)
    values_act, slopes_act, hidden = zip(*(parts for parts, _ in results))
    normed_two = [block for _, blocks in results for block in blocks]

    def apart(flat):
        return [flat[n : n + tokens] for n in range(0, flat.shape[0], tokens)]

    def down_term(i, hidden_part):
        out = BF16 if i else F32
        return apart(out_call([hidden_part], [(down_full, ())], hidden_part.shape[0], 0, out))

    mlp_parts, _ = ring_scatter(down_term, hidden)

    block_out, d_mlp_own, grad_four = by_rows_call(
        end_kernel,
        [*mlp_parts, resid, grad_out[0], gain_rows[2]],
        [(row, BF16), (row, BF16), ((1, width), F32)],
    )

    def contract(i, blocks, last):
        return unit_call(
            contract_kernel,
            blocks,
            [(down_full, ())],
            [values_act[i], slopes_act[i]],
            [BF16, BF16],
        ), list(blocks)

    results = ring_gather(d_mlp_own, contract)
    d_gate, d_up = zip(*(grads for grads, _ in results))
    d_mlp = [block for _, blocks in results for block in blocks]

    def to_owner(full):
        return lax.psum_scatter(full, "fsdp", scatter_dimension=0, tiled=True)

    def grad_up_work(i, state):
        if i == half_ring - 2:
            return state, weight_grad(*state, (0, 2, None))
        if i == half_ring - 3:
            return weight_grad(*state[0], (2, 1, state[1]))
        return state

    def rows_term(i, grads):
        out = BF16 if i else F32
        return apart(out_call(grads, [gate_weight, up_weight], grads[0].shape[0], 0, out))

    d_normed_parts, grad_up_full = ring_scatter(
        rows_term,
        list(zip(d_gate, d_up)),
        grad_up_work,
        (d_up, normed_two),
    )
    d_resid, d_attn_own, grad_two, grad_three = by_rows_call(
        back_kernel,
        [*d_normed_parts, resid, attn_out, grad_out[0], *gain_rows[:2]],
        [(row, F32), (row, BF16), ((1, width), F32), ((1, width), F32)],
    )
    cosines, sines = jnp.tile(cosine, (group, 1)), jnp.tile(sine, (group, 1))
    angles = fixed(group * tokens, HEAD_DIM // 2)
    pair = (2, seqs, tokens, HEAD_DIM)

    def attend_back(chip, d_attn, earlier):
        def at(i):
            return 2 * i + chip

        def half_of(first):
            return pl.BlockSpec((first, 1, tokens, HEAD_DIM), lambda i: (0, at(i), 0, 0))

        by_seq_rows = pl.BlockSpec((tokens, group * HEAD_DIM), lambda i: (at(i), 0))
        return attention_call(
            attend_back_kernel,
            both,
            2,
            at,
            [(queries.shape, BF16)] + [(pair, BF16)] * (n_ctx - 1) + [((1, *pair[1:]), BF16)] * 2,
            [queries, *d_attn, output_full, rows_pos[None, :], key_pos[:, None], cosines, sines],
            [by_seq_rows, fixed(tokens, width), fixed(tokens, width)]
            + [fixed(*output_full.shape), fixed(1, group * tokens), fixed(count, 1)]
            + [angles, angles],
            [by_seq_rows] + [half_of(2)] * (n_ctx - 1) + [half_of(1)] * 2,
            earlier,
        )

    d_attn_far, d_attn_near = far_hop(d_attn_own), near_hop(d_attn_own)
    earlier = attend_back(0, [d_attn_own, d_attn_near], ())
    d_attn_far, earlier, grad_up_full = tie(d_attn_far, earlier, grad_up_full)
    flying["up"] = to_owner(grad_up_full)
    d_attn_last = near_hop(d_attn_far)
    d_query_raw, *d_both = attend_back(1, [d_attn_far, d_attn_last], earlier)
    d_attn = jnp.concatenate([d_attn_own, d_attn_far, d_attn_near, d_attn_last], axis=0)

    def both_of(distance):
        at = max(2 * distance - 1, 0)
        return d_both[at : at + (1 if distance == 0 else 2)]

    def query_work(i, state):
        if i == half_ring - 2:
            return weight_grad(*state[0]), *state[1:]
        if i == half_ring - 3:
            flying["gate"] = to_owner(state[0])
            return weight_grad(*state[1])
        if i == 0:
            flying["down"] = to_owner(state)
            return (
                flying.pop("up"),
                tn(d_query_raw, normed_one).astype(BF16),
                tn(mixed, d_attn).astype(BF16),
            )
        return state

    d_both, state = ring_scatter(
        lambda i, blocks: blocks,
        [both_of(distance) for distance in range(half_ring + 1)],
        query_work,
        ((d_gate, normed_two), (hidden, d_mlp)),
    )
    grad_up, grad_query_full, grad_output_full = state
    d_key_raw, d_value_raw, grad_key_full, grad_value_full = keys_back(
        d_both, cosine, sine, normed_one
    )
    grad_fulls = [grad_query_full, grad_key_full, grad_value_full, grad_output_full]

    def weight_terms(i, fulls):
        if i == half_ring:
            member = ring_member(i)
            return member_rows([(fulls[:2], cols[:2], member), (fulls[2:], cols[2:], member)], BF16)
        ends = [0] if i == 0 else [-i, i]
        return member_rows([(fulls, cols, ring_member(k)) for k in ends], BF16)

    def input_side(i, state):
        if i == half_ring - 1:
            ds, up = state
            kept, sent, grad_one = input_terms(
                ds, [query_full, key_full, value_full], all_rows, scales
            )
            return kept, sent, jnp.concatenate([grad_one, grad_two, grad_three, grad_four], axis=0), up
        if i == half_ring - 2:
            kept, sent, sums, up = state
            sums = add_from(sums, "fsdp", low_masks())
            return kept, near_hop(sent), sums, up.T.astype(F32), flying.pop("gate")
        if i == half_ring - 3:
            kept, near, sums, up, gate = state
            total = kept + near.astype(F32)
            arrived = far_hop(total[tokens:].astype(BF16))
            sums = add_from(sums, "ctx", low_masks())
            return total[:tokens] + arrived.astype(F32), sums, up, gate
        if i == 0:
            d_normed_one, sums, up, gate = state
            d_rows_attn, _ = norm_back(rows_in, gain_one, d_normed_one)
            sums = add_from(sums, "ctx", high_masks())
            return d_resid + d_rows_attn, sums, up, gate.T.astype(F32)
        return state

    grad_all, state = ring_scatter(
        weight_terms,
        [grad_fulls] * (half_ring + 1),
        input_side,
        ((d_query_raw, d_key_raw, d_value_raw), grad_up),
    )
    grad_all = grad_all[0].astype(F32) + (grad_all[1].astype(F32) + grad_all[2].astype(F32))
    grad_in, grad_gains, grad_up, grad_gate = state
    grad_down, grad_all = tie(flying.pop("down"), grad_all)
    grad_down = grad_down.astype(F32)
    grad_query, grad_key, grad_value, grad_output = (
        grad_all[a:b] for a, b in zip(cuts, cuts[1:])
    )
    grad_query, grad_key, grad_value = grad_query.T, grad_key.T, grad_value.T
    grad_gains = lax.dynamic_slice_in_dim(grad_gains, own_place, share, axis=1)
    return (
        block_out[None],
        grad_in[None],
        grad_query,
        grad_key,
        grad_value,
        grad_output,
        grad_gate,
        grad_up,
        grad_down,
        grad_gains[0],
        grad_gains[1],
        grad_gains[2],
        grad_gains[3],
    )


def solution(mesh):
    rows = P("fsdp", "ctx", None)
    columns = P(None, ("fsdp", "ctx"))
    units = P(("fsdp", "ctx"), None)
    gain = P(("ctx", "fsdp"))
    weights = (columns, columns, columns, units, columns, columns, units)
    return jax.shard_map(
        body,
        mesh=mesh,
        in_specs=(rows, P()) + weights + (gain,) * 4 + (rows,),
        out_specs=(rows, rows) + weights + (gain,) * 4,
        check_vma=False,
    )
```

```python
import functools
import math

import jax
import jax.numpy as jnp
from jax import lax
from jax.experimental import pallas as pl
from jax.experimental.pallas import tpu as pltpu
from jax.sharding import PartitionSpec as P

HEAD_DIM = 256
EPS = 1e-06
CAP = 50.0
NEGATIVE = -1e30
BF16 = jnp.bfloat16
F32 = jnp.float32


def ring_order(size):
    return list(range(0, size, 2)) + list(range(size - 1, 0, -2))


def ring_hop(block, step):
    order = ring_order(lax.axis_size("ctx"))
    size = len(order)
    return lax.ppermute(block, "ctx", [(order[i], order[(i + step) % size]) for i in range(size)])


def ring_member(offset):
    size = lax.axis_size("ctx")
    own = lax.axis_index("ctx")
    place = jnp.where(own % 2 == 0, own // 2, size - 1 - own // 2)
    place = (place + offset) % size
    return jnp.where(place < size // 2, 2 * place, 2 * (size - 1 - place) + 1)


def ring_groups():
    half = lax.axis_size("ctx") // 2
    return [[0]] + [[-k, k] for k in range(1, half)] + [[half]]


def tie(*values):
    return lax.optimization_barrier(values)


def ring_moves(i, behind, ahead):
    if i < lax.axis_size("ctx") // 2 - 1:
        return [ring_hop(behind, 1), ring_hop(ahead, -1)]
    middle = behind.shape[0] // 2
    return [ring_hop(behind[:middle], 1), ring_hop(ahead[middle:], -1)]


def ring_gather(own, use, side=None, state=(), first=()):
    half = lax.axis_size("ctx") // 2
    own, state, result = tie(own, state, first)
    blocks, results = [own], []
    behind = ahead = own
    for i in range(half):
        last = i == half - 1
        moved = ring_moves(i, behind, ahead)
        result = use(i, blocks, result)
        if side:
            state = side(i, state)
        moved, result, state = tie(moved, result, state)
        results.append(result)
        if not last:
            blocks = behind, ahead = moved
    results.append(use(half, moved, result))
    return (results, state) if side else results


def add_terms(terms, moved):
    to_behind, to_ahead = terms
    behind, ahead = (block.astype(F32) for block in moved)
    if behind.shape != to_ahead.shape:
        gap = jnp.zeros_like(behind)
        behind = jnp.concatenate([behind, gap], axis=0)
        ahead = jnp.concatenate([gap, ahead], axis=0)
    return [
        (to_ahead.astype(F32) + behind).astype(BF16),
        (to_behind.astype(F32) + ahead).astype(BF16),
    ]


def add_kernel(halves, to_behind_ref, to_ahead_ref, behind_ref, ahead_ref, ahead_out, behind_out):
    behind, ahead = behind_ref[...].astype(F32), ahead_ref[...].astype(F32)
    if halves:
        first = pl.program_id(0) == 0
        behind, ahead = jnp.where(first, behind, 0.0), jnp.where(first, 0.0, ahead)
    ahead_out[...] = (to_ahead_ref[...].astype(F32) + behind).astype(BF16)
    behind_out[...] = (to_behind_ref[...].astype(F32) + ahead).astype(BF16)


def add_terms_here(terms, moved):
    whole, part = terms[0].shape, moved[0].shape
    block = (whole[0] // 2, *whole[1:])
    rest = (0,) * (len(whole) - 1)
    halves = whole != part
    here = pl.BlockSpec(block, lambda i: (i, *rest))
    there = pl.BlockSpec(block, lambda i: (0, *rest)) if halves else here
    return pl.pallas_call(
        functools.partial(add_kernel, halves),
        grid=(2,),
        out_shape=[jax.ShapeDtypeStruct(whole, BF16)] * 2,
        in_specs=[here, here, there, there],
        out_specs=[here, here],
        compiler_params=ROOMY,
        cost_estimate=FREE,
    )(*terms, *moved)


def ring_scatter(term, operands, side=None, state=(), join=add_terms):
    half = lax.axis_size("ctx") // 2
    far = term(half, operands[half])
    if len(far) == 1:
        middle = far[0].shape[0] // 2
        far = [far[0][:middle], far[0][middle:]]
    sums = [part.astype(BF16) for part in far]
    for i in range(half - 1, -1, -1):
        sums, operand, state = tie(sums, operands[i], state)
        moved = [ring_hop(sums[0], 1), ring_hop(sums[1], -1)]
        terms = term(i, operand)
        if side:
            state = side(i, state)
        moved, terms, state = tie(moved, terms, state)
        if i > 0:
            sums = join(terms, moved)
    return (terms[0], *moved), state


def far_hop(block):
    size = lax.axis_size("fsdp")
    return lax.ppermute(block, "fsdp", [(i, i ^ (size // 2)) for i in range(size)])


def near_hop(block):
    size = lax.axis_size("fsdp")
    return lax.ppermute(block, "fsdp", [(i, i ^ 1) for i in range(size)])


def add_from(block, axis, masks):
    size = lax.axis_size(axis)
    routes = [[(i, i ^ mask) for i in range(size)] for mask in masks if mask < size]
    return sum((lax.ppermute(block, axis, route) for route in routes), block)


def low_masks():
    return range(1, 4)


def high_masks():
    return range(4, lax.axis_size("ctx"), 4)


def rms_norm(values, gain):
    return values * lax.rsqrt(jnp.mean(values * values, axis=-1, keepdims=True) + EPS) * gain


def norm_back(values, gain, cotangent):
    scale = lax.rsqrt(jnp.mean(values * values, axis=-1, keepdims=True) + EPS)
    normal = values * scale
    turned = cotangent * gain
    along = jnp.mean(turned * normal, axis=-1, keepdims=True)
    return scale * (turned - normal * along), jnp.sum(cotangent * normal, axis=0)


def rotate(values, cosine, sine):
    middle = values.shape[-1] // 2
    first = values[..., :middle]
    second = values[..., middle:]
    return jnp.concatenate(
        [first * cosine - second * sine, second * cosine + first * sine], axis=-1
    )


def dot(a, b, dims):
    return lax.dot_general(a, b, (dims, ((), ())), preferred_element_type=F32)


def nn(a, b):
    return dot(a, b, ((1,), (0,)))


def nt(a, b):
    return dot(a, b, ((1,), (1,)))


def tn(a, b):
    return dot(a, b, ((0,), (0,)))


def gelu_parts(gate):
    slope = math.sqrt(2.0 / math.pi)
    square = gate * gate
    tanh = jnp.tanh(slope * gate * (1.0 + 0.044715 * square))
    value = 0.5 * gate * (1.0 + tanh)
    inner = slope * (1.0 + 3.0 * 0.044715 * square)
    return value, 0.5 * (1.0 + tanh) + 0.5 * gate * (1.0 - tanh * tanh) * inner


def normed(values):
    scale = lax.rsqrt(jnp.mean(values * values, axis=-1, keepdims=True) + EPS)
    return values * scale, scale


def pulled(values, gain, cotangent):
    normal, scale = normed(values)
    through = cotangent * gain
    along = jnp.mean(through * normal, axis=-1, keepdims=True)
    return scale * (through - normal * along), jnp.sum(cotangent * normal, axis=0, keepdims=True)


def middle_kernel(rows_ref, kept_ref, moved_ref, gain_two_ref, gain_three_ref, *outs):
    attn_out_ref, resid_ref, normed_two_ref = outs
    attn_out = kept_ref[...] + moved_ref[...].astype(F32)
    resid = rows_ref[...].astype(F32) + normed(attn_out)[0] * gain_two_ref[...]
    attn_out_ref[...] = attn_out
    resid_ref[...] = resid
    normed_two_ref[...] = (normed(resid)[0] * gain_three_ref[...]).astype(BF16)


def end_kernel(term_ref, behind_ref, ahead_ref, resid_ref, grad_ref, gain_ref, *outs):
    block_out_ref, d_mlp_ref, grad_gain_ref = outs
    mlp_out = term_ref[...] + (behind_ref[...].astype(F32) + ahead_ref[...].astype(F32))
    block_out_ref[...] = (resid_ref[...] + normed(mlp_out)[0] * gain_ref[...]).astype(BF16)
    d_mlp, grad_gain_ref[...] = pulled(mlp_out, gain_ref[...], grad_ref[...].astype(F32))
    d_mlp_ref[...] = d_mlp.astype(BF16)


def back_kernel(
    term_ref,
    behind_ref,
    ahead_ref,
    resid_ref,
    attn_out_ref,
    grad_ref,
    gain_two_ref,
    gain_three_ref,
    d_resid_ref,
    d_attn_ref,
    grad_two_ref,
    grad_three_ref,
):
    d_normed = term_ref[...] + (behind_ref[...].astype(F32) + ahead_ref[...].astype(F32))
    d_rows, grad_three_ref[...] = pulled(resid_ref[...], gain_three_ref[...], d_normed)
    d_resid = grad_ref[...].astype(F32) + d_rows
    d_resid_ref[...] = d_resid
    d_attn, grad_two_ref[...] = pulled(attn_out_ref[...], gain_two_ref[...], d_resid)
    d_attn_ref[...] = d_attn.astype(BF16)


def by_rows_call(kernel, args, outs):
    return pl.pallas_call(
        kernel,
        out_shape=[jax.ShapeDtypeStruct(*out) for out in outs],
        compiler_params=pltpu.CompilerParams(vmem_limit_bytes=24 << 20),
        cost_estimate=FREE,
    )(*args)


def input_kernel(seqs, refs_in, refs_w, rows_ref, scale_ref, kept_ref, sent_ref, gain_ref):
    total = sum(nn(d[...], w[...]) for d, w in zip(refs_in, refs_w))
    half = total.shape[0] // 2
    kept_ref[...] = total[:half]
    sent_ref[...] = total[half:].astype(BF16)
    normal = rows_ref[...].astype(F32) * scale_ref[...]
    gain_ref[...] = jnp.sum(total * normal, axis=0, keepdims=True)


def input_terms(ds, weights, rows, scale):
    count, width = rows.shape
    half = count // 2
    tile = tile_of(width, 768)

    def kernel(*refs):
        input_kernel(0, refs[:3], refs[3:6], *refs[6:])

    by_cols = lambda i: (0, i)
    return pl.pallas_call(
        kernel,
        grid=(width // tile,),
        out_shape=[
            jax.ShapeDtypeStruct((half, width), F32),
            jax.ShapeDtypeStruct((half, width), BF16),
            jax.ShapeDtypeStruct((1, width), F32),
        ],
        in_specs=[pl.BlockSpec(d.shape, lambda i: (0, 0)) for d in ds]
        + [pl.BlockSpec((w.shape[0], tile), by_cols) for w in weights]
        + [pl.BlockSpec((count, tile), by_cols), pl.BlockSpec((count, 1), lambda i: (0, 0))],
        out_specs=[
            pl.BlockSpec((half, tile), by_cols),
            pl.BlockSpec((half, tile), by_cols),
            pl.BlockSpec((1, tile), by_cols),
        ],
        compiler_params=ROOMY,
        cost_estimate=FREE,
    )(*ds, *weights, rows, scale)


def stacked(flat):
    heads = flat.shape[1] // HEAD_DIM
    return jnp.concatenate(
        [flat[:, h * HEAD_DIM : (h + 1) * HEAD_DIM] for h in range(heads)], axis=0
    )


def side_by_side(tall, rows):
    return jnp.concatenate(
        [tall[i : i + rows] for i in range(0, tall.shape[0], rows)], axis=1
    )


FREE = pl.CostEstimate(flops=0, bytes_accessed=0, transcendentals=0)
ROOMY = pltpu.CompilerParams(vmem_limit_bytes=56 << 20)


def blank(shapes):
    return pl.pallas_call(
        lambda *refs: None,
        out_shape=[jax.ShapeDtypeStruct(shape, BF16) for shape in shapes],
        out_specs=[pl.BlockSpec(memory_space=pl.ANY)] * len(shapes),
    )()


def place_kernel(cols, n_blocks, members_ref, *refs):
    blocks, outs = refs[:n_blocks], refs[n_blocks + len(cols) :]

    for n, block in enumerate(blocks):

        @pl.when(pl.program_id(0) == n)
        def _(block=block):
            start = 0
            for out, count in zip(outs, cols):
                out[...] = block[start : start + count]
                start += count


def place_rows(fulls, blocks, members, cols):
    width = blocks[0].shape[1]
    if any(count % 16 for count in cols):
        for block, member in zip(blocks, members):
            start = 0
            for m, count in enumerate(cols):
                part = block[start : start + count]
                fulls[m] = lax.dynamic_update_slice_in_dim(fulls[m], part, member * count, axis=0)
                start += count
        return fulls
    n_blocks = len(blocks)
    return pl.pallas_call(
        functools.partial(place_kernel, cols, n_blocks),
        grid_spec=pltpu.PrefetchScalarGridSpec(
            num_scalar_prefetch=1,
            grid=(n_blocks,),
            in_specs=[pl.BlockSpec(block.shape, lambda i, m: (0, 0)) for block in blocks]
            + [pl.BlockSpec(memory_space=pl.ANY)] * len(fulls),
            out_specs=[pl.BlockSpec((count, width), lambda i, m: (m[i], 0)) for count in cols],
        ),
        out_shape=[jax.ShapeDtypeStruct(full.shape, full.dtype) for full in fulls],
        input_output_aliases={1 + n_blocks + m: m for m in range(len(fulls))},
        cost_estimate=FREE,
    )(jnp.stack(members), *blocks, *fulls)


def put_kernel(n_blocks, *refs):
    for n in range(n_blocks):

        @pl.when(pl.program_id(0) == n)
        def _(n=n):
            refs[-1][...] = refs[n][...]


def put_blocks(full, blocks, at, along):
    shape = blocks[0].shape
    where = (lambda i: (i, at, 0)) if along == 0 else (lambda i: (0, at + i, 0))
    return pl.pallas_call(
        functools.partial(put_kernel, len(blocks)),
        grid=(len(blocks),),
        out_shape=jax.ShapeDtypeStruct(full.shape, full.dtype),
        in_specs=[pl.BlockSpec(shape, lambda i: (0, 0, 0))] * len(blocks)
        + [pl.BlockSpec(memory_space=pl.ANY)],
        out_specs=pl.BlockSpec(shape, where),
        input_output_aliases={len(blocks): 0},
        cost_estimate=FREE,
    )(*blocks, full)


def tile_of(count, tile):
    return tile if count % tile == 0 else count


def stack_rows(refs):
    return jnp.concatenate([ref[...] for ref in refs], axis=0) if len(refs) > 1 else refs[0][...]


def weight_grad_kernel(groups, blocks, *refs):
    units, rows, out_ref, all_rows = refs[:groups], refs[groups : groups + blocks], refs[-2], refs[-1]

    @pl.when(pl.program_id(0) == 0)
    def _():
        at = 0
        for row in rows:
            all_rows[at : at + row.shape[0]] = row[...]
            at += row.shape[0]

    out_ref[...] = tn(stack_rows(units), all_rows[...]).astype(BF16)


def weight_grad(units, rows, part=None):
    count, width = units[0].shape[1], rows[0].shape[1]
    total = sum(row.shape[0] for row in rows)
    tile = tile_of(count, 384)
    first, tiles, before = part or (0, count // tile, None)
    first, tiles = min(first, count // tile - 1), min(tiles, count // tile)
    held = [] if before is None else [before]
    return pl.pallas_call(
        functools.partial(weight_grad_kernel, len(units), len(rows)),
        grid=(tiles,),
        out_shape=jax.ShapeDtypeStruct((count, width), BF16),
        in_specs=[pl.BlockSpec((unit.shape[0], tile), lambda i: (0, first + i)) for unit in units]
        + [pl.BlockSpec(row.shape, lambda i: (0, 0)) for row in rows]
        + [pl.BlockSpec(memory_space=pl.ANY)] * len(held),
        out_specs=pl.BlockSpec((tile, width), lambda i: (first + i, 0)),
        scratch_shapes=[pltpu.VMEM((total, width), BF16)],
        input_output_aliases={len(units) + len(rows): 0} if held else {},
        compiler_params=ROOMY,
        cost_estimate=FREE,
    )(*units, *rows, *held)


def expand_kernel(blocks, *refs):
    rows = stack_rows(refs[:blocks])
    gate_ref, up_ref, value_ref, slope_ref, hidden_ref = refs[blocks:]
    gate, up = nt(rows, gate_ref[0]), nt(rows, up_ref[0])
    value, slope = gelu_parts(gate)
    value_ref[...] = value
    slope_ref[...] = up * slope
    hidden_ref[...] = (value * up).astype(BF16)


def contract_kernel(blocks, *refs):
    rows = stack_rows(refs[:blocks])
    down_ref, value_ref, slope_ref, d_gate_ref, d_up_ref = refs[blocks:]
    d_hidden = nt(rows, down_ref[...])
    d_gate_ref[...] = (d_hidden * slope_ref[...]).astype(BF16)
    d_up_ref[...] = (d_hidden * value_ref[...]).astype(BF16)


def unit_call(kernel, rows, weights, units, outs):
    count, width = weights[0][0].shape[-2:]
    total = sum(row.shape[0] for row in rows)
    tile = tile_of(count, 384)
    weight_specs = [
        pl.BlockSpec((1,) * len(at) + (tile, width), lambda i, at=at: (*at, i, 0))
        for _, at in weights
    ]
    flat = pl.BlockSpec((total, tile), lambda i: (0, i))
    return pl.pallas_call(
        functools.partial(kernel, len(rows)),
        grid=(count // tile,),
        out_shape=[jax.ShapeDtypeStruct((total, count), out) for out in outs],
        in_specs=[pl.BlockSpec(row.shape, lambda i: (0, 0)) for row in rows]
        + weight_specs
        + [flat] * len(units),
        out_specs=[flat] * len(outs),
        compiler_params=pltpu.CompilerParams(vmem_limit_bytes=24 << 20),
        cost_estimate=FREE,
    )(*rows, *(weight for weight, _ in weights), *units)


def out_kernel(pairs, *refs):
    ins, weights, outs = refs[:pairs], refs[pairs : 2 * pairs], refs[2 * pairs :]
    total = sum(nn(a[...], w[...].reshape(w.shape[-2:])) for a, w in zip(ins, weights))
    rows = outs[0].shape[0]
    for n, out in enumerate(outs):
        out[...] = total[n * rows : (n + 1) * rows].astype(out.dtype)


def out_call(ins, weights, rows, out):
    count, width = weights[0][0].shape[-2:]
    blocks = ins[0].shape[0] // rows
    tile = tile_of(width, 768)
    return pl.pallas_call(
        functools.partial(out_kernel, len(ins)),
        grid=(width // tile,),
        out_shape=[jax.ShapeDtypeStruct((rows, width), out)] * blocks,
        in_specs=[pl.BlockSpec(a.shape, lambda i: (0, 0)) for a in ins]
        + [
            pl.BlockSpec((1,) * len(lead) + (count, tile), lambda i, lead=lead: (*lead, 0, i))
            for _, lead in weights
        ],
        out_specs=[pl.BlockSpec((rows, tile), lambda i: (0, i))] * blocks,
        compiler_params=pltpu.CompilerParams(vmem_limit_bytes=24 << 20),
        cost_estimate=FREE,
    )(*ins, *(weight for weight, _ in weights))


def gather_kernel(counts, *refs):
    ins, outs = refs[len(counts) : -len(counts)], refs[-len(counts) :]
    for out, cols in zip(outs, counts):
        start = 0
        for count in cols:
            out[start : start + count] = ins[0][...].astype(out.dtype)
            start += count
            ins = ins[1:]


def member_rows(parts, dtype):
    width = parts[0][0][0].shape[1]
    counts = [cols for _, cols, _ in parts]
    if any(count % 16 for cols in counts for count in cols):
        return [
            jnp.concatenate(
                [
                    lax.dynamic_slice_in_dim(full, member * c, c, axis=0)
                    for full, c in zip(arrays, cols)
                ],
                axis=0,
            ).astype(dtype)
            for arrays, cols, member in parts
        ]
    return pl.pallas_call(
        functools.partial(gather_kernel, counts),
        grid_spec=pltpu.PrefetchScalarGridSpec(
            num_scalar_prefetch=len(parts),
            grid=(1,),
            in_specs=[
                pl.BlockSpec((count, width), lambda i, *m, side=side: (m[side][0], 0))
                for side, cols in enumerate(counts)
                for count in cols
            ],
            out_specs=[pl.BlockSpec((sum(cols), width), lambda i, *m: (0, 0)) for cols in counts],
        ),
        out_shape=[jax.ShapeDtypeStruct((sum(cols), width), dtype) for cols in counts],
        compiler_params=ROOMY,
        cost_estimate=FREE,
    )(
        *(member.reshape(1) for _, _, member in parts),
        *(array for arrays, _, _ in parts for array in arrays),
    )


def keys_back_kernel(term_ref, behind_ref, ahead_ref, cosine_ref, sine_ref, rows_ref, *outs):
    d_keys_ref, d_values_ref, grad_keys_ref, grad_values_ref = outs
    total = term_ref[...].astype(F32) + (
        behind_ref[...].astype(F32) + ahead_ref[...].astype(F32)
    )
    d_keys = rotate(total[0], cosine_ref[...], -sine_ref[...]).astype(BF16)
    d_keys = d_keys.reshape(-1, HEAD_DIM)
    d_values = total[1].astype(BF16).reshape(-1, HEAD_DIM)
    d_keys_ref[...] = d_keys
    d_values_ref[...] = d_values
    grad_keys_ref[...] = tn(d_keys, rows_ref[...]).astype(BF16)
    grad_values_ref[...] = tn(d_values, rows_ref[...]).astype(BF16)


def keys_back(parts, cosine, sine, rows):
    count, width = rows.shape
    tile = tile_of(width, 768)
    whole = pl.BlockSpec(parts[0].shape, lambda i: (0, 0, 0, 0))
    flat = pl.BlockSpec((count, HEAD_DIM), lambda i: (0, 0))
    angle = pl.BlockSpec(cosine.shape, lambda i: (0, 0))
    tall = pl.BlockSpec((HEAD_DIM, tile), lambda i: (0, i))
    return pl.pallas_call(
        keys_back_kernel,
        grid=(width // tile,),
        out_shape=[jax.ShapeDtypeStruct((count, HEAD_DIM), BF16)] * 2
        + [jax.ShapeDtypeStruct((HEAD_DIM, width), BF16)] * 2,
        in_specs=[whole] * 3 + [angle] * 2 + [pl.BlockSpec((count, tile), lambda i: (0, i))],
        out_specs=[flat] * 2 + [tall] * 2,
        compiler_params=ROOMY,
        cost_estimate=FREE,
    )(*parts, cosine, sine, rows)


def turned(raw, cosine, sine):
    return jnp.concatenate(
        [
            rotate(raw[:, at : at + HEAD_DIM], cosine, sine)
            for at in range(0, raw.shape[1], HEAD_DIM)
        ],
        axis=1,
    )


def queries_kernel(rows_ref, weight_ref, cosine_ref, sine_ref, out_ref):
    raw = nt(rows_ref[...], weight_ref[...])
    out_ref[...] = (turned(raw, cosine_ref[...], sine_ref[...]) * HEAD_DIM ** (-0.5)).astype(BF16)


def keys_kernel(rows_ref, key_ref, value_ref, cosine_ref, sine_ref, out_ref):
    rows = rows_ref[...]
    out_ref[0, 0] = rotate(nt(rows, key_ref[...]), cosine_ref[...], sine_ref[...]).astype(BF16)
    out_ref[1, 0] = nt(rows, value_ref[...]).astype(BF16)


def project(kernel, rows, weights, cosine, sine, out, out_spec):
    tokens, width = cosine.shape[0], rows.shape[1]

    def whole(array):
        return pl.BlockSpec(array.shape, lambda i: (0, 0))

    return pl.pallas_call(
        kernel,
        grid=(rows.shape[0] // tokens,),
        out_shape=jax.ShapeDtypeStruct(out, BF16),
        in_specs=[pl.BlockSpec((tokens, width), lambda i: (i, 0))]
        + [whole(array) for array in (*weights, cosine, sine)],
        out_specs=out_spec,
        compiler_params=pltpu.CompilerParams(vmem_limit_bytes=16 << 20),
        cost_estimate=FREE,
    )(rows, *weights, cosine, sine)


def attend_kernel(keys_ref, values_ref, queries_ref, query_pos_ref, key_pos_ref, mixed_ref):
    queries = stacked(queries_ref[...])
    tanh = jnp.tanh(nt(queries, keys_ref[0]) * (1.0 / CAP))
    weights = jnp.where(key_pos_ref[...] <= query_pos_ref[...], jnp.exp(CAP * tanh), 0.0)
    total = jnp.sum(weights, axis=1, keepdims=True)
    mixed = nn(weights.astype(BF16), values_ref[0]) / total
    mixed_ref[...] = side_by_side(mixed.astype(BF16), queries_ref.shape[0])


def attend_back_kernel(
    keys_ref,
    values_ref,
    queries_ref,
    d_attn_ref,
    d_attn_next_ref,
    output_ref,
    query_pos_ref,
    key_pos_ref,
    cosine_ref,
    sine_ref,
    *refs,
):
    blocks = key_pos_ref.shape[0] // queries_ref.shape[0]
    d_queries_ref, *d_both_refs = refs[-blocks - 2 :]
    rows = queries_ref.shape[0]
    queries = stacked(queries_ref[...])
    d_attn = jnp.where(pl.program_id(0) == 0, d_attn_ref[...], d_attn_next_ref[...])
    d_mixed = stacked(nt(d_attn, output_ref[...]).astype(BF16))
    keys = keys_ref[0]
    tanh = jnp.tanh(nt(keys, queries) * (1.0 / CAP))
    weights = jnp.where(key_pos_ref[...] <= query_pos_ref[...], jnp.exp(CAP * tanh), 0.0)
    probs = weights * (1.0 / jnp.sum(weights, axis=0, keepdims=True))
    d_values = nn(probs.astype(BF16), d_mixed).astype(BF16)
    for n, out in enumerate(d_both_refs[:-2]):
        out[1, 0] = d_values[n * rows : (n + 1) * rows]
    d_both_refs[-1][0, 0] = d_values[(blocks - 1) * rows :]
    d_probs = nt(values_ref[0], d_mixed)
    delta = jnp.sum(probs * d_probs, axis=0, keepdims=True)
    d_scores = (probs * (d_probs - delta) * (1.0 - tanh * tanh)).astype(BF16)
    d_keys = nn(d_scores, queries).astype(BF16)
    for n, out in enumerate(d_both_refs[:-2]):
        out[0, 0] = d_keys[n * rows : (n + 1) * rows]
    d_both_refs[-2][0, 0] = d_keys[(blocks - 1) * rows :]
    d_queries = tn(d_scores, keys) * HEAD_DIM ** (-0.5)
    d_queries = rotate(d_queries, cosine_ref[...], -sine_ref[...])
    d_queries_ref[...] = side_by_side(d_queries.astype(BF16), rows)


def attention_call(kernel, both, seqs, at, outs, args, specs, out_specs, earlier=()):
    count = both.shape[1]
    total = both.shape[0] // 2
    held = len(args) + 2
    return pl.pallas_call(
        kernel,
        grid=(seqs,),
        out_shape=[jax.ShapeDtypeStruct(*out) for out in outs],
        in_specs=[
            pl.BlockSpec((1, count, HEAD_DIM), lambda i: (at(i), 0, 0)),
            pl.BlockSpec((1, count, HEAD_DIM), lambda i: (at(i) + total, 0, 0)),
        ]
        + specs
        + [pl.BlockSpec(memory_space=pl.ANY)] * len(earlier),
        out_specs=out_specs,
        input_output_aliases={held + n: n for n in range(len(earlier))},
        compiler_params=ROOMY,
        cost_estimate=FREE,
    )(both, both, *args, *earlier)


def body(
    block_in,
    stretch_order,
    weight_query,
    weight_key,
    weight_value,
    weight_output,
    weight_gate,
    weight_up,
    weight_down,
    gain_preattn,
    gain_postattn,
    gain_premlp,
    gain_postmlp,
    grad_out,
):
    n_ctx, n_fsdp = lax.axis_size("ctx"), lax.axis_size("fsdp")
    own_ctx, own_fsdp = lax.axis_index("ctx"), lax.axis_index("fsdp")
    rows_in = block_in[0].astype(F32)
    tokens, width = rows_in.shape
    half = tokens // 2
    half_ring = n_ctx // 2
    groups = ring_groups()
    members = [[ring_member(k) for k in group] for group in groups]

    steps = jnp.arange(HEAD_DIM // 2, dtype=F32)
    inverse = jnp.exp(steps * (-2.0 * math.log(10000.0) / HEAD_DIM))

    def positions(member):
        starts = lax.dynamic_slice_in_dim(stretch_order, member, 1, axis=0)[0]
        return (starts[:, None] * half + jnp.arange(half, dtype=jnp.int32)[None, :]).reshape(-1)

    query_pos = positions(own_ctx)
    key_pos = [jnp.concatenate([positions(m) for m in group]) for group in members]
    angle = query_pos.astype(F32)[:, None] * inverse[None, :]
    cosine, sine = jnp.cos(angle), jnp.sin(angle)

    gains = jnp.stack([gain_preattn, gain_postattn, gain_premlp, gain_postmlp])
    share = gains.shape[1]
    own_place = (own_ctx * n_fsdp + own_fsdp) * share
    gains = lax.dynamic_update_slice_in_dim(jnp.zeros((4, width), F32), gains, own_place, axis=1)

    cols = [weight_query.shape[1], weight_key.shape[1], weight_value.shape[1]]
    cols.append(weight_output.shape[0])
    cuts = [sum(cols[:i]) for i in range(len(cols) + 1)]

    def place_group(i, blocks, fulls, cols):
        ends = [0] if i == 0 else [-i, i]
        return list(place_rows(list(fulls), list(blocks), [ring_member(k) for k in ends], cols))

    def place_far(blocks, fulls, cols):
        member = [ring_member(half_ring)]
        return [
            place_rows([full], [block], member, [c])[0]
            for full, block, c in zip(fulls, blocks, cols)
        ]

    flying = {}

    def prepare(i, state):
        if i == 0:
            gate_own, up_own = state
            rows = [block_in[0], far_hop(block_in[0]), near_hop(block_in[0])]
            own = jnp.stack([gate_own.T, up_own.T])
            rows[2], part = tie(rows[2], gains)
            return rows, add_from(part, "fsdp", low_masks()), own
        if i == 1:
            rows, sums, own = state
            flying["gate_up"] = lax.all_gather(own, "fsdp", axis=1, tiled=True)
            rows = [*rows, near_hop(rows[1])]
            return rows, add_from(sums, "ctx", low_masks())
        if i == 2:
            rows, sums = state
            return jnp.concatenate(rows, axis=0), add_from(sums, "ctx", high_masks())
        if i == half_ring - 1:
            rows, sums = state
            long = rows.astype(F32)
            scales = lax.rsqrt(jnp.mean(long * long, axis=-1, keepdims=True) + EPS)
            return rows, scales, (long * scales * sums[0]).astype(BF16), sums
        return state

    kv_cols, qo_cols = cols[1:3], [cols[0], cols[3]]
    kv_own = jnp.concatenate([weight_key.T, weight_value.T], axis=0)
    qo_own = jnp.concatenate([weight_query.T, weight_output], axis=0)
    kv_own, qo_own, state = tie(kv_own, qo_own, (weight_gate, weight_up))
    kv, qo, kv_group, qo_group = [kv_own] * 2, [qo_own] * 2, [kv_own], [qo_own]
    kv_full = blank([(c * n_ctx, width) for c in kv_cols])
    qo_full = blank([(c * n_ctx, width) for c in qo_cols])
    late = half_ring - 2
    for i in range(half_ring):
        kv_moved = ring_moves(i, *kv)
        qo_moved = ring_moves(i, *qo) if i < late else qo
        kv_full = place_group(i, kv_group, kv_full, kv_cols)
        if i <= late:
            qo_full = place_group(i, qo_group, qo_full, qo_cols)
        state = prepare(i, state)
        kv_moved, qo_moved, kv_full, qo_full, state = tie(kv_moved, qo_moved, kv_full, qo_full, state)
        kv = kv_group = kv_moved
        qo = qo_group = qo_moved
    all_rows, scales, normed_one, gains = state
    gain_one, gain_two, gain_three, gain_four = gains[0], gains[1], gains[2], gains[3]

    seqs = n_fsdp
    group = weight_query.shape[1] * n_ctx // HEAD_DIM

    by_rows = pl.BlockSpec((tokens, group * HEAD_DIM), lambda i: (i, 0))
    qo_moved = ring_moves(late, *qo)
    key_full, value_full = place_far(kv, kv_full, kv_cols)
    both_own = project(
        keys_kernel,
        normed_one,
        [key_full, value_full],
        cosine,
        sine,
        (2, seqs, tokens, HEAD_DIM),
        pl.BlockSpec((2, 1, tokens, HEAD_DIM), lambda i: (0, i, 0, 0)),
    ).reshape(2 * seqs, tokens, HEAD_DIM)
    qo, both_own = tie(qo_moved, both_own)

    def take_keys(i, blocks, both):
        return put_blocks(both, list(blocks), max(2 * i - 1, 0), 0 if i == half_ring else 1)

    def keys_side(i, state):
        if i == 0:
            qo, qo_full = state
            moved = ring_moves(half_ring - 1, *qo)
            return moved, place_group(half_ring - 1, qo, qo_full, qo_cols)
        if i == 1:
            query_full, output_full = place_far(*state, qo_cols)
            queries = project(
                queries_kernel,
                normed_one,
                [query_full],
                cosine,
                sine,
                (seqs * tokens, group * HEAD_DIM),
                by_rows,
            )
            return queries, query_full, output_full, flying.pop("gate_up"), weight_down
        if i == 2:
            *kept, own = state
            flying["down"] = lax.all_gather(own, "fsdp", axis=0, tiled=True)
            return kept
        return state

    count = tokens * n_ctx
    results, (queries, query_full, output_full, gate_up) = ring_gather(
        both_own,
        take_keys,
        keys_side,
        (qo, qo_full),
        blank([(2 * seqs, count, HEAD_DIM)])[0],
    )
    both = results[-1]
    rows_pos = jnp.tile(query_pos, group)
    key_pos = jnp.concatenate(key_pos)
    def fixed(*shape):
        return pl.BlockSpec(shape, lambda i: (0, 0))

    (mixed,) = attention_call(
        attend_kernel,
        both,
        seqs,
        lambda i: i,
        [(queries.shape, BF16)],
        [queries, rows_pos[:, None], key_pos[None, :]],
        [by_rows, fixed(group * tokens, 1), fixed(1, count)],
        [by_rows],
    )

    def by_seq(flat):
        return [flat[i * tokens : (i + 1) * tokens] for i in range(seqs)]

    def fold(terms):
        moved = near_hop(jnp.stack([term.astype(BF16) for term in terms[2:]]))
        return terms[0] + moved[0].astype(F32), (terms[1] + moved[1].astype(F32)).astype(BF16)

    kept, sent = fold(by_seq(nn(mixed, output_full)))
    row = (tokens, width)
    gain_rows = [gain[None, :] for gain in (gain_two, gain_three, gain_four)]
    attn_out, resid, normed_two_own = by_rows_call(
        middle_kernel,
        [block_in[0], kept, far_hop(sent), *gain_rows[:2]],
        [(row, F32), (row, F32), (row, BF16)],
    )

    gate_weight, up_weight = (gate_up, (0,)), (gate_up, (1,))

    def expand(i, blocks, last):
        weights = [gate_weight, up_weight]
        return unit_call(expand_kernel, blocks, weights, [], [F32, F32, BF16]), list(blocks)

    def finish_down(i, state):
        return flying.pop("down") if i == 0 else state

    results, down_full = ring_gather(normed_two_own, expand, finish_down)
    values_act, slopes_act, hidden = zip(*(parts for parts, _ in results))
    normed_two = [block for _, blocks in results for block in blocks]

    def down_term(i, hidden_part):
        out = BF16 if i else F32
        return out_call([hidden_part], [(down_full, ())], tokens, out)

    mlp_parts, _ = ring_scatter(down_term, hidden)

    block_out, d_mlp_own, grad_four = by_rows_call(
        end_kernel,
        [*mlp_parts, resid, grad_out[0], gain_rows[2]],
        [(row, BF16), (row, BF16), ((1, width), F32)],
    )

    def contract(i, blocks, last):
        return unit_call(
            contract_kernel,
            blocks,
            [(down_full, ())],
            [values_act[i], slopes_act[i]],
            [BF16, BF16],
        ), list(blocks)

    results = ring_gather(d_mlp_own, contract)
    d_gate, d_up = zip(*(grads for grads, _ in results))
    d_mlp = [block for _, blocks in results for block in blocks]

    def to_owner(full):
        return lax.psum_scatter(full, "fsdp", scatter_dimension=0, tiled=True)

    def grad_up_work(i, state):
        if i == half_ring - 2:
            return state, weight_grad(*state, (0, 2, None))
        return state

    def rows_term(i, grads):
        out = BF16 if i else F32
        return out_call(list(grads), [gate_weight, up_weight], tokens, out)

    d_normed_parts, (sides, grad_up_part) = ring_scatter(
        rows_term,
        list(zip(d_gate, d_up)),
        grad_up_work,
        (d_up, normed_two),
    )
    d_resid, d_attn_own, grad_two, grad_three = by_rows_call(
        back_kernel,
        [*d_normed_parts, resid, attn_out, grad_out[0], *gain_rows[:2]],
        [(row, F32), (row, BF16), ((1, width), F32), ((1, width), F32)],
    )
    cosines, sines = jnp.tile(cosine, (group, 1)), jnp.tile(sine, (group, 1))
    angles = fixed(group * tokens, HEAD_DIM // 2)
    pair = (2, seqs, tokens, HEAD_DIM)

    def attend_back(chip, d_attn, earlier):
        def at(i):
            return 2 * i + chip

        def half_of(first):
            return pl.BlockSpec((first, 1, tokens, HEAD_DIM), lambda i: (0, at(i), 0, 0))

        by_seq_rows = pl.BlockSpec((tokens, group * HEAD_DIM), lambda i: (at(i), 0))
        return attention_call(
            attend_back_kernel,
            both,
            2,
            at,
            [(queries.shape, BF16)] + [(pair, BF16)] * (n_ctx - 1) + [((1, *pair[1:]), BF16)] * 2,
            [queries, *d_attn, output_full, rows_pos[None, :], key_pos[:, None], cosines, sines],
            [by_seq_rows, fixed(tokens, width), fixed(tokens, width)]
            + [fixed(*output_full.shape), fixed(1, group * tokens), fixed(count, 1)]
            + [angles, angles],
            [by_seq_rows] + [half_of(2)] * (n_ctx - 1) + [half_of(1)] * 2,
            earlier,
        )

    d_attn_far, d_attn_near = far_hop(d_attn_own), near_hop(d_attn_own)
    earlier = attend_back(0, [d_attn_own, d_attn_near], ())
    grad_up_part, _ = tie(grad_up_part, d_attn_near)
    grad_up_full = weight_grad(*sides, (2, 1, grad_up_part))
    d_attn_far, earlier, grad_up_full = tie(d_attn_far, earlier, grad_up_full)
    flying["up"] = to_owner(grad_up_full)
    d_attn_last = near_hop(d_attn_far)
    d_query_raw, *d_both = attend_back(1, [d_attn_far, d_attn_last], earlier)
    d_attn = jnp.concatenate([d_attn_own, d_attn_far, d_attn_near, d_attn_last], axis=0)

    def both_of(distance):
        at = max(2 * distance - 1, 0)
        return d_both[at : at + (1 if distance == 0 else 2)]

    def query_work(i, state):
        if i == half_ring - 2:
            return weight_grad(*state[0]), *state[1:]
        if i == half_ring - 3:
            flying["gate"] = to_owner(state[0])
            return weight_grad(*state[1])
        if i == 0:
            flying["down"] = to_owner(state)
            return (
                flying.pop("up"),
                tn(d_query_raw, normed_one).astype(BF16),
                tn(mixed, d_attn).astype(BF16),
            )
        return state

    d_both, state = ring_scatter(
        lambda i, blocks: blocks,
        [both_of(distance) for distance in range(half_ring + 1)],
        query_work,
        ((d_gate, normed_two), (hidden, d_mlp)),
        add_terms_here,
    )
    grad_up, grad_query_full, grad_output_full = state
    d_key_raw, d_value_raw, grad_key_full, grad_value_full = keys_back(
        d_both, cosine, sine, normed_one
    )
    grad_fulls = [grad_query_full, grad_key_full, grad_value_full, grad_output_full]

    def weight_terms(i, fulls):
        if i == half_ring:
            member = ring_member(i)
            return member_rows([(fulls[:2], cols[:2], member), (fulls[2:], cols[2:], member)], BF16)
        ends = [0] if i == 0 else [-i, i]
        return member_rows([(fulls, cols, ring_member(k)) for k in ends], BF16)

    def input_side(i, state):
        if i == half_ring - 1:
            ds, up = state
            kept, sent, grad_one = input_terms(
                ds, [query_full, key_full, value_full], all_rows, scales
            )
            return kept, sent, jnp.concatenate([grad_one, grad_two, grad_three, grad_four], axis=0), up
        if i == half_ring - 2:
            kept, sent, sums, up = state
            sums = add_from(sums, "fsdp", low_masks())
            return kept, near_hop(sent), sums, up.T.astype(F32), flying.pop("gate")
        if i == half_ring - 3:
            kept, near, sums, up, gate = state
            total = kept + near.astype(F32)
            arrived = far_hop(total[tokens:].astype(BF16))
            sums = add_from(sums, "ctx", low_masks())
            return total[:tokens] + arrived.astype(F32), sums, up, gate
        if i == 0:
            d_normed_one, sums, up, gate = state
            d_rows_attn, _ = norm_back(rows_in, gain_one, d_normed_one)
            sums = add_from(sums, "ctx", high_masks())
            return d_resid + d_rows_attn, sums, up, gate.T.astype(F32)
        return state

    grad_all, state = ring_scatter(
        weight_terms,
        [grad_fulls] * (half_ring + 1),
        input_side,
        ((d_query_raw, d_key_raw, d_value_raw), grad_up),
    )
    grad_all = grad_all[0].astype(F32) + (grad_all[1].astype(F32) + grad_all[2].astype(F32))
    grad_in, grad_gains, grad_up, grad_gate = state
    grad_down, grad_all = tie(flying.pop("down"), grad_all)
    grad_down = grad_down.astype(F32)
    grad_query, grad_key, grad_value, grad_output = (
        grad_all[a:b] for a, b in zip(cuts, cuts[1:])
    )
    grad_query, grad_key, grad_value = grad_query.T, grad_key.T, grad_value.T
    grad_gains = lax.dynamic_slice_in_dim(grad_gains, own_place, share, axis=1)
    return (
        block_out[None],
        grad_in[None],
        grad_query,
        grad_key,
        grad_value,
        grad_output,
        grad_gate,
        grad_up,
        grad_down,
        grad_gains[0],
        grad_gains[1],
        grad_gains[2],
        grad_gains[3],
    )


def solution(mesh):
    rows = P("fsdp", "ctx", None)
    columns = P(None, ("fsdp", "ctx"))
    units = P(("fsdp", "ctx"), None)
    gain = P(("ctx", "fsdp"))
    weights = (columns, columns, columns, units, columns, columns, units)
    return jax.shard_map(
        body,
        mesh=mesh,
        in_specs=(rows, P()) + weights + (gain,) * 4 + (rows,),
        out_specs=(rows, rows) + weights + (gain,) * 4,
        check_vma=False,
    )
```

```python
import functools
import math

import jax
import jax.numpy as jnp
from jax import lax
from jax.experimental import pallas as pl
from jax.experimental.pallas import tpu as pltpu
from jax.sharding import PartitionSpec as P

HEAD_DIM = 256
EPS = 1e-06
CAP = 50.0
NEGATIVE = -1e30
BF16 = jnp.bfloat16
F32 = jnp.float32


def ring_order(size):
    return list(range(0, size, 2)) + list(range(size - 1, 0, -2))


def ring_hop(block, step):
    order = ring_order(lax.axis_size("ctx"))
    size = len(order)
    return lax.ppermute(block, "ctx", [(order[i], order[(i + step) % size]) for i in range(size)])


def ring_member(offset):
    size = lax.axis_size("ctx")
    own = lax.axis_index("ctx")
    place = jnp.where(own % 2 == 0, own // 2, size - 1 - own // 2)
    place = (place + offset) % size
    return jnp.where(place < size // 2, 2 * place, 2 * (size - 1 - place) + 1)


def ring_groups():
    half = lax.axis_size("ctx") // 2
    return [[0]] + [[-k, k] for k in range(1, half)] + [[half]]


def tie(*values):
    return lax.optimization_barrier(values)


def ring_moves(i, behind, ahead):
    if i < lax.axis_size("ctx") // 2 - 1:
        return [ring_hop(behind, 1), ring_hop(ahead, -1)]
    middle = behind.shape[0] // 2
    return [ring_hop(behind[:middle], 1), ring_hop(ahead[middle:], -1)]


def ring_gather(own, use, side=None, state=(), first=()):
    half = lax.axis_size("ctx") // 2
    own, state, result = tie(own, state, first)
    blocks, results = [own], []
    behind = ahead = own
    for i in range(half):
        last = i == half - 1
        moved = ring_moves(i, behind, ahead)
        result = use(i, blocks, result)
        if side:
            state = side(i, state)
        moved, result, state = tie(moved, result, state)
        results.append(result)
        if not last:
            blocks = behind, ahead = moved
    results.append(use(half, moved, result))
    return (results, state) if side else results


def add_terms(terms, moved):
    to_behind, to_ahead = terms
    behind, ahead = (block.astype(F32) for block in moved)
    if behind.shape != to_ahead.shape:
        gap = jnp.zeros_like(behind)
        behind = jnp.concatenate([behind, gap], axis=0)
        ahead = jnp.concatenate([gap, ahead], axis=0)
    return [
        (to_ahead.astype(F32) + behind).astype(BF16),
        (to_behind.astype(F32) + ahead).astype(BF16),
    ]


def add_kernel(halves, to_behind_ref, to_ahead_ref, behind_ref, ahead_ref, ahead_out, behind_out):
    behind, ahead = behind_ref[...].astype(F32), ahead_ref[...].astype(F32)
    if halves:
        first = pl.program_id(0) == 0
        behind, ahead = jnp.where(first, behind, 0.0), jnp.where(first, 0.0, ahead)
    ahead_out[...] = (to_ahead_ref[...].astype(F32) + behind).astype(BF16)
    behind_out[...] = (to_behind_ref[...].astype(F32) + ahead).astype(BF16)


def add_terms_here(terms, moved):
    whole, part = terms[0].shape, moved[0].shape
    block = (whole[0] // 2, *whole[1:])
    rest = (0,) * (len(whole) - 1)
    halves = whole != part
    here = pl.BlockSpec(block, lambda i: (i, *rest))
    there = pl.BlockSpec(block, lambda i: (0, *rest)) if halves else here
    return pl.pallas_call(
        functools.partial(add_kernel, halves),
        grid=(2,),
        out_shape=[jax.ShapeDtypeStruct(whole, BF16)] * 2,
        in_specs=[here, here, there, there],
        out_specs=[here, here],
        compiler_params=ROOMY,
        cost_estimate=FREE,
    )(*terms, *moved)


def ring_scatter(term, operands, side=None, state=(), join=add_terms):
    half = lax.axis_size("ctx") // 2
    far = term(half, operands[half])
    if len(far) == 1:
        middle = far[0].shape[0] // 2
        far = [far[0][:middle], far[0][middle:]]
    sums = [part.astype(BF16) for part in far]
    for i in range(half - 1, -1, -1):
        sums, operand, state = tie(sums, operands[i], state)
        moved = [ring_hop(sums[0], 1), ring_hop(sums[1], -1)]
        terms = term(i, operand)
        if side:
            state = side(i, state)
        moved, terms, state = tie(moved, terms, state)
        if i > 0:
            sums = join(terms, moved)
    return (terms[0], *moved), state


def far_hop(block):
    size = lax.axis_size("fsdp")
    return lax.ppermute(block, "fsdp", [(i, i ^ (size // 2)) for i in range(size)])


def near_hop(block):
    size = lax.axis_size("fsdp")
    return lax.ppermute(block, "fsdp", [(i, i ^ 1) for i in range(size)])


def add_from(block, axis, masks):
    size = lax.axis_size(axis)
    routes = [[(i, i ^ mask) for i in range(size)] for mask in masks if mask < size]
    return sum((lax.ppermute(block, axis, route) for route in routes), block)


def low_masks():
    return range(1, 4)


def high_masks():
    return range(4, lax.axis_size("ctx"), 4)


def rms_norm(values, gain):
    return values * lax.rsqrt(jnp.mean(values * values, axis=-1, keepdims=True) + EPS) * gain


def norm_back(values, gain, cotangent):
    scale = lax.rsqrt(jnp.mean(values * values, axis=-1, keepdims=True) + EPS)
    normal = values * scale
    turned = cotangent * gain
    along = jnp.mean(turned * normal, axis=-1, keepdims=True)
    return scale * (turned - normal * along), jnp.sum(cotangent * normal, axis=0)


def rotate(values, cosine, sine):
    middle = values.shape[-1] // 2
    first = values[..., :middle]
    second = values[..., middle:]
    return jnp.concatenate(
        [first * cosine - second * sine, second * cosine + first * sine], axis=-1
    )


def dot(a, b, dims):
    return lax.dot_general(a, b, (dims, ((), ())), preferred_element_type=F32)


def nn(a, b):
    return dot(a, b, ((1,), (0,)))


def nt(a, b):
    return dot(a, b, ((1,), (1,)))


def tn(a, b):
    return dot(a, b, ((0,), (0,)))


def gelu_parts(gate):
    slope = math.sqrt(2.0 / math.pi)
    square = gate * gate
    tanh = jnp.tanh(slope * gate * (1.0 + 0.044715 * square))
    value = 0.5 * gate * (1.0 + tanh)
    inner = slope * (1.0 + 3.0 * 0.044715 * square)
    return value, 0.5 * (1.0 + tanh) + 0.5 * gate * (1.0 - tanh * tanh) * inner


def normed(values):
    scale = lax.rsqrt(jnp.mean(values * values, axis=-1, keepdims=True) + EPS)
    return values * scale, scale


def pulled(values, gain, cotangent):
    normal, scale = normed(values)
    through = cotangent * gain
    along = jnp.mean(through * normal, axis=-1, keepdims=True)
    return scale * (through - normal * along), jnp.sum(cotangent * normal, axis=0, keepdims=True)


def middle_kernel(rows_ref, kept_ref, moved_ref, gain_two_ref, gain_three_ref, *outs):
    attn_out_ref, resid_ref, normed_two_ref = outs
    attn_out = kept_ref[...] + moved_ref[...].astype(F32)
    resid = rows_ref[...].astype(F32) + normed(attn_out)[0] * gain_two_ref[...]
    attn_out_ref[...] = attn_out
    resid_ref[...] = resid
    normed_two_ref[...] = (normed(resid)[0] * gain_three_ref[...]).astype(BF16)


def end_kernel(term_ref, behind_ref, ahead_ref, resid_ref, grad_ref, gain_ref, *outs):
    block_out_ref, d_mlp_ref, grad_gain_ref = outs
    mlp_out = term_ref[...] + (behind_ref[...].astype(F32) + ahead_ref[...].astype(F32))
    block_out_ref[...] = (resid_ref[...] + normed(mlp_out)[0] * gain_ref[...]).astype(BF16)
    d_mlp, grad_gain_ref[...] = pulled(mlp_out, gain_ref[...], grad_ref[...].astype(F32))
    d_mlp_ref[...] = d_mlp.astype(BF16)


def back_kernel(
    term_ref,
    behind_ref,
    ahead_ref,
    resid_ref,
    attn_out_ref,
    grad_ref,
    gain_two_ref,
    gain_three_ref,
    d_resid_ref,
    d_attn_ref,
    grad_two_ref,
    grad_three_ref,
):
    d_normed = term_ref[...] + (behind_ref[...].astype(F32) + ahead_ref[...].astype(F32))
    d_rows, grad_three_ref[...] = pulled(resid_ref[...], gain_three_ref[...], d_normed)
    d_resid = grad_ref[...].astype(F32) + d_rows
    d_resid_ref[...] = d_resid
    d_attn, grad_two_ref[...] = pulled(attn_out_ref[...], gain_two_ref[...], d_resid)
    d_attn_ref[...] = d_attn.astype(BF16)


def by_rows_call(kernel, args, outs):
    return pl.pallas_call(
        kernel,
        out_shape=[jax.ShapeDtypeStruct(*out) for out in outs],
        compiler_params=pltpu.CompilerParams(vmem_limit_bytes=24 << 20),
        cost_estimate=FREE,
    )(*args)


def input_kernel(seqs, refs_in, refs_w, rows_ref, scale_ref, kept_ref, sent_ref, gain_ref):
    total = sum(nn(d[...], w[...]) for d, w in zip(refs_in, refs_w))
    half = total.shape[0] // 2
    kept_ref[...] = total[:half]
    sent_ref[...] = total[half:].astype(BF16)
    normal = rows_ref[...].astype(F32) * scale_ref[...]
    gain_ref[...] = jnp.sum(total * normal, axis=0, keepdims=True)


def input_terms(ds, weights, rows, scale):
    count, width = rows.shape
    half = count // 2
    tile = tile_of(width, 768)

    def kernel(*refs):
        input_kernel(0, refs[:3], refs[3:6], *refs[6:])

    by_cols = lambda i: (0, i)
    return pl.pallas_call(
        kernel,
        grid=(width // tile,),
        out_shape=[
            jax.ShapeDtypeStruct((half, width), F32),
            jax.ShapeDtypeStruct((half, width), BF16),
            jax.ShapeDtypeStruct((1, width), F32),
        ],
        in_specs=[pl.BlockSpec(d.shape, lambda i: (0, 0)) for d in ds]
        + [pl.BlockSpec((w.shape[0], tile), by_cols) for w in weights]
        + [pl.BlockSpec((count, tile), by_cols), pl.BlockSpec((count, 1), lambda i: (0, 0))],
        out_specs=[
            pl.BlockSpec((half, tile), by_cols),
            pl.BlockSpec((half, tile), by_cols),
            pl.BlockSpec((1, tile), by_cols),
        ],
        compiler_params=ROOMY,
        cost_estimate=FREE,
    )(*ds, *weights, rows, scale)


def stacked(flat):
    heads = flat.shape[1] // HEAD_DIM
    return jnp.concatenate(
        [flat[:, h * HEAD_DIM : (h + 1) * HEAD_DIM] for h in range(heads)], axis=0
    )


def side_by_side(tall, rows):
    return jnp.concatenate(
        [tall[i : i + rows] for i in range(0, tall.shape[0], rows)], axis=1
    )


FREE = pl.CostEstimate(flops=0, bytes_accessed=0, transcendentals=0)
ROOMY = pltpu.CompilerParams(vmem_limit_bytes=56 << 20)


def blank(shapes):
    return pl.pallas_call(
        lambda *refs: None,
        out_shape=[jax.ShapeDtypeStruct(shape, BF16) for shape in shapes],
        out_specs=[pl.BlockSpec(memory_space=pl.ANY)] * len(shapes),
    )()


def place_kernel(cols, n_blocks, members_ref, *refs):
    blocks, outs = refs[:n_blocks], refs[n_blocks + len(cols) :]

    for n, block in enumerate(blocks):

        @pl.when(pl.program_id(0) == n)
        def _(block=block):
            start = 0
            for out, count in zip(outs, cols):
                out[...] = block[start : start + count]
                start += count


def place_rows(fulls, blocks, members, cols):
    width = blocks[0].shape[1]
    if any(count % 16 for count in cols):
        for block, member in zip(blocks, members):
            start = 0
            for m, count in enumerate(cols):
                part = block[start : start + count]
                fulls[m] = lax.dynamic_update_slice_in_dim(fulls[m], part, member * count, axis=0)
                start += count
        return fulls
    n_blocks = len(blocks)
    return pl.pallas_call(
        functools.partial(place_kernel, cols, n_blocks),
        grid_spec=pltpu.PrefetchScalarGridSpec(
            num_scalar_prefetch=1,
            grid=(n_blocks,),
            in_specs=[pl.BlockSpec(block.shape, lambda i, m: (0, 0)) for block in blocks]
            + [pl.BlockSpec(memory_space=pl.ANY)] * len(fulls),
            out_specs=[pl.BlockSpec((count, width), lambda i, m: (m[i], 0)) for count in cols],
        ),
        out_shape=[jax.ShapeDtypeStruct(full.shape, full.dtype) for full in fulls],
        input_output_aliases={1 + n_blocks + m: m for m in range(len(fulls))},
        cost_estimate=FREE,
    )(jnp.stack(members), *blocks, *fulls)


def put_kernel(n_blocks, *refs):
    for n in range(n_blocks):

        @pl.when(pl.program_id(0) == n)
        def _(n=n):
            refs[-1][...] = refs[n][...]


def put_blocks(full, blocks, at, along):
    shape = blocks[0].shape
    where = (lambda i: (i, at, 0)) if along == 0 else (lambda i: (0, at + i, 0))
    return pl.pallas_call(
        functools.partial(put_kernel, len(blocks)),
        grid=(len(blocks),),
        out_shape=jax.ShapeDtypeStruct(full.shape, full.dtype),
        in_specs=[pl.BlockSpec(shape, lambda i: (0, 0, 0))] * len(blocks)
        + [pl.BlockSpec(memory_space=pl.ANY)],
        out_specs=pl.BlockSpec(shape, where),
        input_output_aliases={len(blocks): 0},
        cost_estimate=FREE,
    )(*blocks, full)


def tile_of(count, tile):
    return tile if count % tile == 0 else count


def stack_rows(refs):
    return jnp.concatenate([ref[...] for ref in refs], axis=0) if len(refs) > 1 else refs[0][...]


def weight_grad_kernel(groups, blocks, *refs):
    units, rows, out_ref, all_rows = refs[:groups], refs[groups : groups + blocks], refs[-2], refs[-1]

    @pl.when(pl.program_id(0) == 0)
    def _():
        at = 0
        for row in rows:
            all_rows[at : at + row.shape[0]] = row[...]
            at += row.shape[0]

    out_ref[...] = tn(stack_rows(units), all_rows[...]).astype(BF16)


def weight_grad(units, rows, part=None):
    count, width = units[0].shape[1], rows[0].shape[1]
    total = sum(row.shape[0] for row in rows)
    tile = tile_of(count, 384)
    first, tiles, before = part or (0, count // tile, None)
    first, tiles = min(first, count // tile - 1), min(tiles, count // tile)
    held = [] if before is None else [before]
    return pl.pallas_call(
        functools.partial(weight_grad_kernel, len(units), len(rows)),
        grid=(tiles,),
        out_shape=jax.ShapeDtypeStruct((count, width), BF16),
        in_specs=[pl.BlockSpec((unit.shape[0], tile), lambda i: (0, first + i)) for unit in units]
        + [pl.BlockSpec(row.shape, lambda i: (0, 0)) for row in rows]
        + [pl.BlockSpec(memory_space=pl.ANY)] * len(held),
        out_specs=pl.BlockSpec((tile, width), lambda i: (first + i, 0)),
        scratch_shapes=[pltpu.VMEM((total, width), BF16)],
        input_output_aliases={len(units) + len(rows): 0} if held else {},
        compiler_params=ROOMY,
        cost_estimate=FREE,
    )(*units, *rows, *held)


def expand_kernel(blocks, *refs):
    rows = stack_rows(refs[:blocks])
    gate_ref, up_ref, value_ref, slope_ref, hidden_ref = refs[blocks:]
    gate, up = nt(rows, gate_ref[0]), nt(rows, up_ref[0])
    value, slope = gelu_parts(gate)
    value_ref[...] = value
    slope_ref[...] = up * slope
    hidden_ref[...] = (value * up).astype(BF16)


def contract_kernel(blocks, *refs):
    rows = stack_rows(refs[:blocks])
    down_ref, value_ref, slope_ref, d_gate_ref, d_up_ref = refs[blocks:]
    d_hidden = nt(rows, down_ref[...])
    d_gate_ref[...] = (d_hidden * slope_ref[...]).astype(BF16)
    d_up_ref[...] = (d_hidden * value_ref[...]).astype(BF16)


def unit_call(kernel, rows, weights, units, outs):
    count, width = weights[0][0].shape[-2:]
    total = sum(row.shape[0] for row in rows)
    tile = tile_of(count, 384)
    weight_specs = [
        pl.BlockSpec((1,) * len(at) + (tile, width), lambda i, at=at: (*at, i, 0))
        for _, at in weights
    ]
    flat = pl.BlockSpec((total, tile), lambda i: (0, i))
    return pl.pallas_call(
        functools.partial(kernel, len(rows)),
        grid=(count // tile,),
        out_shape=[jax.ShapeDtypeStruct((total, count), out) for out in outs],
        in_specs=[pl.BlockSpec(row.shape, lambda i: (0, 0)) for row in rows]
        + weight_specs
        + [flat] * len(units),
        out_specs=[flat] * len(outs),
        compiler_params=pltpu.CompilerParams(vmem_limit_bytes=24 << 20),
        cost_estimate=FREE,
    )(*rows, *(weight for weight, _ in weights), *units)


def out_kernel(pairs, *refs):
    ins, weights, outs = refs[:pairs], refs[pairs : 2 * pairs], refs[2 * pairs :]
    total = sum(nn(a[...], w[...].reshape(w.shape[-2:])) for a, w in zip(ins, weights))
    rows = outs[0].shape[0]
    for n, out in enumerate(outs):
        out[...] = total[n * rows : (n + 1) * rows].astype(out.dtype)


def out_call(ins, weights, rows, out):
    count, width = weights[0][0].shape[-2:]
    blocks = ins[0].shape[0] // rows
    tile = tile_of(width, 768)
    return pl.pallas_call(
        functools.partial(out_kernel, len(ins)),
        grid=(width // tile,),
        out_shape=[jax.ShapeDtypeStruct((rows, width), out)] * blocks,
        in_specs=[pl.BlockSpec(a.shape, lambda i: (0, 0)) for a in ins]
        + [
            pl.BlockSpec((1,) * len(lead) + (count, tile), lambda i, lead=lead: (*lead, 0, i))
            for _, lead in weights
        ],
        out_specs=[pl.BlockSpec((rows, tile), lambda i: (0, i))] * blocks,
        compiler_params=pltpu.CompilerParams(vmem_limit_bytes=24 << 20),
        cost_estimate=FREE,
    )(*ins, *(weight for weight, _ in weights))


def gather_kernel(counts, *refs):
    ins, outs = refs[len(counts) : -len(counts)], refs[-len(counts) :]
    for out, cols in zip(outs, counts):
        start = 0
        for count in cols:
            out[start : start + count] = ins[0][...].astype(out.dtype)
            start += count
            ins = ins[1:]


def member_rows(parts, dtype):
    width = parts[0][0][0].shape[1]
    counts = [cols for _, cols, _ in parts]
    if any(count % 16 for cols in counts for count in cols):
        return [
            jnp.concatenate(
                [
                    lax.dynamic_slice_in_dim(full, member * c, c, axis=0)
                    for full, c in zip(arrays, cols)
                ],
                axis=0,
            ).astype(dtype)
            for arrays, cols, member in parts
        ]
    return pl.pallas_call(
        functools.partial(gather_kernel, counts),
        grid_spec=pltpu.PrefetchScalarGridSpec(
            num_scalar_prefetch=len(parts),
            grid=(1,),
            in_specs=[
                pl.BlockSpec((count, width), lambda i, *m, side=side: (m[side][0], 0))
                for side, cols in enumerate(counts)
                for count in cols
            ],
            out_specs=[pl.BlockSpec((sum(cols), width), lambda i, *m: (0, 0)) for cols in counts],
        ),
        out_shape=[jax.ShapeDtypeStruct((sum(cols), width), dtype) for cols in counts],
        compiler_params=ROOMY,
        cost_estimate=FREE,
    )(
        *(member.reshape(1) for _, _, member in parts),
        *(array for arrays, _, _ in parts for array in arrays),
    )


def keys_back_kernel(term_ref, behind_ref, ahead_ref, cosine_ref, sine_ref, rows_ref, *outs):
    d_keys_ref, d_values_ref, grad_keys_ref, grad_values_ref = outs
    total = term_ref[...].astype(F32) + (
        behind_ref[...].astype(F32) + ahead_ref[...].astype(F32)
    )
    d_keys = rotate(total[0], cosine_ref[...], -sine_ref[...]).astype(BF16)
    d_keys = d_keys.reshape(-1, HEAD_DIM)
    d_values = total[1].astype(BF16).reshape(-1, HEAD_DIM)
    d_keys_ref[...] = d_keys
    d_values_ref[...] = d_values
    grad_keys_ref[...] = tn(d_keys, rows_ref[...]).astype(BF16)
    grad_values_ref[...] = tn(d_values, rows_ref[...]).astype(BF16)


def keys_back(parts, cosine, sine, rows):
    count, width = rows.shape
    tile = tile_of(width, 768)
    whole = pl.BlockSpec(parts[0].shape, lambda i: (0, 0, 0, 0))
    flat = pl.BlockSpec((count, HEAD_DIM), lambda i: (0, 0))
    angle = pl.BlockSpec(cosine.shape, lambda i: (0, 0))
    tall = pl.BlockSpec((HEAD_DIM, tile), lambda i: (0, i))
    return pl.pallas_call(
        keys_back_kernel,
        grid=(width // tile,),
        out_shape=[jax.ShapeDtypeStruct((count, HEAD_DIM), BF16)] * 2
        + [jax.ShapeDtypeStruct((HEAD_DIM, width), BF16)] * 2,
        in_specs=[whole] * 3 + [angle] * 2 + [pl.BlockSpec((count, tile), lambda i: (0, i))],
        out_specs=[flat] * 2 + [tall] * 2,
        compiler_params=ROOMY,
        cost_estimate=FREE,
    )(*parts, cosine, sine, rows)


def turned(raw, cosine, sine):
    return jnp.concatenate(
        [
            rotate(raw[:, at : at + HEAD_DIM], cosine, sine)
            for at in range(0, raw.shape[1], HEAD_DIM)
        ],
        axis=1,
    )


def queries_kernel(rows_ref, weight_ref, cosine_ref, sine_ref, out_ref):
    raw = nt(rows_ref[...], weight_ref[...])
    out_ref[...] = (turned(raw, cosine_ref[...], sine_ref[...]) * HEAD_DIM ** (-0.5)).astype(BF16)


def keys_kernel(rows_ref, key_ref, value_ref, cosine_ref, sine_ref, out_ref):
    rows = rows_ref[...]
    out_ref[0, 0] = rotate(nt(rows, key_ref[...]), cosine_ref[...], sine_ref[...]).astype(BF16)
    out_ref[1, 0] = nt(rows, value_ref[...]).astype(BF16)


def project(kernel, rows, weights, cosine, sine, out, out_spec):
    tokens, width = cosine.shape[0], rows.shape[1]

    def whole(array):
        return pl.BlockSpec(array.shape, lambda i: (0, 0))

    return pl.pallas_call(
        kernel,
        grid=(rows.shape[0] // tokens,),
        out_shape=jax.ShapeDtypeStruct(out, BF16),
        in_specs=[pl.BlockSpec((tokens, width), lambda i: (i, 0))]
        + [whole(array) for array in (*weights, cosine, sine)],
        out_specs=out_spec,
        compiler_params=pltpu.CompilerParams(vmem_limit_bytes=16 << 20),
        cost_estimate=FREE,
    )(rows, *weights, cosine, sine)


def attend_kernel(keys_ref, values_ref, queries_ref, query_pos_ref, key_pos_ref, mixed_ref):
    queries = stacked(queries_ref[...])
    tanh = jnp.tanh(nt(queries, keys_ref[0]) * (1.0 / CAP))
    weights = jnp.where(key_pos_ref[...] <= query_pos_ref[...], jnp.exp(CAP * tanh), 0.0)
    total = jnp.sum(weights, axis=1, keepdims=True)
    mixed = nn(weights.astype(BF16), values_ref[0]) / total
    mixed_ref[...] = side_by_side(mixed.astype(BF16), queries_ref.shape[0])


def attend_back_kernel(
    keys_ref,
    values_ref,
    queries_ref,
    d_attn_ref,
    d_attn_next_ref,
    output_ref,
    query_pos_ref,
    key_pos_ref,
    cosine_ref,
    sine_ref,
    *refs,
):
    blocks = key_pos_ref.shape[0] // queries_ref.shape[0]
    d_queries_ref, *d_both_refs = refs[-blocks - 2 :]
    rows = queries_ref.shape[0]
    queries = stacked(queries_ref[...])
    d_attn = jnp.where(pl.program_id(0) == 0, d_attn_ref[...], d_attn_next_ref[...])
    d_mixed = stacked(nt(d_attn, output_ref[...]).astype(BF16))
    keys = keys_ref[0]
    tanh = jnp.tanh(nt(keys, queries) * (1.0 / CAP))
    weights = jnp.where(key_pos_ref[...] <= query_pos_ref[...], jnp.exp(CAP * tanh), 0.0)
    probs = weights * (1.0 / jnp.sum(weights, axis=0, keepdims=True))
    d_values = nn(probs.astype(BF16), d_mixed).astype(BF16)
    for n, out in enumerate(d_both_refs[:-2]):
        out[1, 0] = d_values[n * rows : (n + 1) * rows]
    d_both_refs[-1][0, 0] = d_values[(blocks - 1) * rows :]
    d_probs = nt(values_ref[0], d_mixed)
    delta = jnp.sum(probs * d_probs, axis=0, keepdims=True)
    d_scores = (probs * (d_probs - delta) * (1.0 - tanh * tanh)).astype(BF16)
    d_keys = nn(d_scores, queries).astype(BF16)
    for n, out in enumerate(d_both_refs[:-2]):
        out[0, 0] = d_keys[n * rows : (n + 1) * rows]
    d_both_refs[-2][0, 0] = d_keys[(blocks - 1) * rows :]
    d_queries = tn(d_scores, keys) * HEAD_DIM ** (-0.5)
    d_queries = rotate(d_queries, cosine_ref[...], -sine_ref[...])
    d_queries_ref[...] = side_by_side(d_queries.astype(BF16), rows)


def attention_call(kernel, both, seqs, at, outs, args, specs, out_specs, earlier=()):
    count = both.shape[1]
    total = both.shape[0] // 2
    held = len(args) + 2
    return pl.pallas_call(
        kernel,
        grid=(seqs,),
        out_shape=[jax.ShapeDtypeStruct(*out) for out in outs],
        in_specs=[
            pl.BlockSpec((1, count, HEAD_DIM), lambda i: (at(i), 0, 0)),
            pl.BlockSpec((1, count, HEAD_DIM), lambda i: (at(i) + total, 0, 0)),
        ]
        + specs
        + [pl.BlockSpec(memory_space=pl.ANY)] * len(earlier),
        out_specs=out_specs,
        input_output_aliases={held + n: n for n in range(len(earlier))},
        compiler_params=ROOMY,
        cost_estimate=FREE,
    )(both, both, *args, *earlier)


def body(
    block_in,
    stretch_order,
    weight_query,
    weight_key,
    weight_value,
    weight_output,
    weight_gate,
    weight_up,
    weight_down,
    gain_preattn,
    gain_postattn,
    gain_premlp,
    gain_postmlp,
    grad_out,
):
    n_ctx, n_fsdp = lax.axis_size("ctx"), lax.axis_size("fsdp")
    own_ctx, own_fsdp = lax.axis_index("ctx"), lax.axis_index("fsdp")
    rows_in = block_in[0].astype(F32)
    tokens, width = rows_in.shape
    half = tokens // 2
    half_ring = n_ctx // 2
    groups = ring_groups()
    members = [[ring_member(k) for k in group] for group in groups]

    steps = jnp.arange(HEAD_DIM // 2, dtype=F32)
    inverse = jnp.exp(steps * (-2.0 * math.log(10000.0) / HEAD_DIM))

    def positions(member):
        starts = lax.dynamic_slice_in_dim(stretch_order, member, 1, axis=0)[0]
        return (starts[:, None] * half + jnp.arange(half, dtype=jnp.int32)[None, :]).reshape(-1)

    query_pos = positions(own_ctx)
    key_pos = [jnp.concatenate([positions(m) for m in group]) for group in members]
    angle = query_pos.astype(F32)[:, None] * inverse[None, :]
    cosine, sine = jnp.cos(angle), jnp.sin(angle)

    gains = jnp.stack([gain_preattn, gain_postattn, gain_premlp, gain_postmlp])
    share = gains.shape[1]
    own_place = (own_ctx * n_fsdp + own_fsdp) * share
    gains = lax.dynamic_update_slice_in_dim(jnp.zeros((4, width), F32), gains, own_place, axis=1)

    cols = [weight_query.shape[1], weight_key.shape[1], weight_value.shape[1]]
    cols.append(weight_output.shape[0])
    cuts = [sum(cols[:i]) for i in range(len(cols) + 1)]

    def place_group(i, blocks, fulls, cols):
        ends = [0] if i == 0 else [-i, i]
        return list(place_rows(list(fulls), list(blocks), [ring_member(k) for k in ends], cols))

    def place_far(blocks, fulls, cols):
        member = [ring_member(half_ring)]
        return [
            place_rows([full], [block], member, [c])[0]
            for full, block, c in zip(fulls, blocks, cols)
        ]

    flying = {}

    def prepare(i, state):
        if i == 0:
            gate_own, up_own = state
            rows = [block_in[0], far_hop(block_in[0]), near_hop(block_in[0])]
            own = jnp.stack([gate_own.T, up_own.T])
            rows[2], part = tie(rows[2], gains)
            return rows, add_from(part, "fsdp", low_masks()), own
        if i == 1:
            rows, sums, own = state
            flying["gate_up"] = lax.all_gather(own, "fsdp", axis=1, tiled=True)
            rows = [*rows, near_hop(rows[1])]
            return rows, add_from(sums, "ctx", low_masks())
        if i == 2:
            rows, sums = state
            return jnp.concatenate(rows, axis=0), add_from(sums, "ctx", high_masks())
        if i == half_ring - 1:
            rows, sums = state
            long = rows.astype(F32)
            scales = lax.rsqrt(jnp.mean(long * long, axis=-1, keepdims=True) + EPS)
            return rows, scales, (long * scales * sums[0]).astype(BF16), sums
        return state

    kv_cols, qo_cols = cols[1:3], [cols[0], cols[3]]
    kv_own = jnp.concatenate([weight_key.T, weight_value.T], axis=0)
    qo_own = jnp.concatenate([weight_query.T, weight_output], axis=0)
    kv_own, qo_own, state = tie(kv_own, qo_own, (weight_gate, weight_up))
    kv, qo, kv_group, qo_group = [kv_own] * 2, [qo_own] * 2, [kv_own], [qo_own]
    kv_full = blank([(c * n_ctx, width) for c in kv_cols])
    qo_full = blank([(c * n_ctx, width) for c in qo_cols])
    late = half_ring - 2
    for i in range(half_ring):
        kv_moved = ring_moves(i, *kv)
        qo_moved = ring_moves(i, *qo) if i < late else qo
        kv_full = place_group(i, kv_group, kv_full, kv_cols)
        if i <= late:
            qo_full = place_group(i, qo_group, qo_full, qo_cols)
        state = prepare(i, state)
        kv_moved, qo_moved, kv_full, qo_full, state = tie(kv_moved, qo_moved, kv_full, qo_full, state)
        kv = kv_group = kv_moved
        qo = qo_group = qo_moved
    all_rows, scales, normed_one, gains = state
    gain_one, gain_two, gain_three, gain_four = gains[0], gains[1], gains[2], gains[3]

    seqs = n_fsdp
    group = weight_query.shape[1] * n_ctx // HEAD_DIM

    by_rows = pl.BlockSpec((tokens, group * HEAD_DIM), lambda i: (i, 0))
    qo_moved = ring_moves(late, *qo)
    key_full, value_full = place_far(kv, kv_full, kv_cols)
    both_own = project(
        keys_kernel,
        normed_one,
        [key_full, value_full],
        cosine,
        sine,
        (2, seqs, tokens, HEAD_DIM),
        pl.BlockSpec((2, 1, tokens, HEAD_DIM), lambda i: (0, i, 0, 0)),
    ).reshape(2 * seqs, tokens, HEAD_DIM)
    qo, both_own = tie(qo_moved, both_own)

    def take_keys(i, blocks, both):
        return put_blocks(both, list(blocks), max(2 * i - 1, 0), 0 if i == half_ring else 1)

    def keys_side(i, state):
        if i == 0:
            qo, qo_full = state
            moved = ring_moves(half_ring - 1, *qo)
            return moved, place_group(half_ring - 1, qo, qo_full, qo_cols)
        if i == 1:
            query_full, output_full = place_far(*state, qo_cols)
            queries = project(
                queries_kernel,
                normed_one,
                [query_full],
                cosine,
                sine,
                (seqs * tokens, group * HEAD_DIM),
                by_rows,
            )
            return queries, query_full, output_full, flying.pop("gate_up"), weight_down
        if i == 2:
            *kept, own = state
            flying["down"] = lax.all_gather(own, "fsdp", axis=0, tiled=True)
            return kept
        return state

    count = tokens * n_ctx
    results, (queries, query_full, output_full, gate_up) = ring_gather(
        both_own,
        take_keys,
        keys_side,
        (qo, qo_full),
        blank([(2 * seqs, count, HEAD_DIM)])[0],
    )
    both = results[-1]
    rows_pos = jnp.tile(query_pos, group)
    key_pos = jnp.concatenate(key_pos)
    def fixed(*shape):
        return pl.BlockSpec(shape, lambda i: (0, 0))

    (mixed,) = attention_call(
        attend_kernel,
        both,
        seqs,
        lambda i: i,
        [(queries.shape, BF16)],
        [queries, rows_pos[:, None], key_pos[None, :]],
        [by_rows, fixed(group * tokens, 1), fixed(1, count)],
        [by_rows],
    )

    def by_seq(flat):
        return [flat[i * tokens : (i + 1) * tokens] for i in range(seqs)]

    def fold(terms):
        moved = near_hop(jnp.stack([term.astype(BF16) for term in terms[2:]]))
        return terms[0] + moved[0].astype(F32), (terms[1] + moved[1].astype(F32)).astype(BF16)

    kept, sent = fold(by_seq(nn(mixed, output_full)))
    row = (tokens, width)
    gain_rows = [gain[None, :] for gain in (gain_two, gain_three, gain_four)]
    attn_out, resid, normed_two_own = by_rows_call(
        middle_kernel,
        [block_in[0], kept, far_hop(sent), *gain_rows[:2]],
        [(row, F32), (row, F32), (row, BF16)],
    )

    gate_weight, up_weight = (gate_up, (0,)), (gate_up, (1,))

    def expand(i, blocks, last):
        weights = [gate_weight, up_weight]
        return unit_call(expand_kernel, blocks, weights, [], [F32, F32, BF16]), list(blocks)

    def finish_down(i, state):
        return flying.pop("down") if i == 0 else state

    results, down_full = ring_gather(normed_two_own, expand, finish_down)
    values_act, slopes_act, hidden = zip(*(parts for parts, _ in results))
    normed_two = [block for _, blocks in results for block in blocks]

    def down_term(i, hidden_part):
        out = BF16 if i else F32
        return out_call([hidden_part], [(down_full, ())], tokens, out)

    mlp_parts, _ = ring_scatter(down_term, hidden)

    block_out, d_mlp_own, grad_four = by_rows_call(
        end_kernel,
        [*mlp_parts, resid, grad_out[0], gain_rows[2]],
        [(row, BF16), (row, BF16), ((1, width), F32)],
    )

    def contract(i, blocks, last):
        return unit_call(
            contract_kernel,
            blocks,
            [(down_full, ())],
            [values_act[i], slopes_act[i]],
            [BF16, BF16],
        ), list(blocks)

    results = ring_gather(d_mlp_own, contract)
    d_gate, d_up = zip(*(grads for grads, _ in results))
    d_mlp = [block for _, blocks in results for block in blocks]

    def to_owner(full):
        return lax.psum_scatter(full, "fsdp", scatter_dimension=0, tiled=True)

    def grad_up_work(i, state):
        if i == half_ring - 2:
            return state, weight_grad(*state, (0, 2, None))
        return state

    def rows_term(i, grads):
        out = BF16 if i else F32
        return out_call(list(grads), [gate_weight, up_weight], tokens, out)

    d_normed_parts, (sides, grad_up_part) = ring_scatter(
        rows_term,
        list(zip(d_gate, d_up)),
        grad_up_work,
        (d_up, normed_two),
    )
    d_resid, d_attn_own, grad_two, grad_three = by_rows_call(
        back_kernel,
        [*d_normed_parts, resid, attn_out, grad_out[0], *gain_rows[:2]],
        [(row, F32), (row, BF16), ((1, width), F32), ((1, width), F32)],
    )
    cosines, sines = jnp.tile(cosine, (group, 1)), jnp.tile(sine, (group, 1))
    angles = fixed(group * tokens, HEAD_DIM // 2)
    pair = (2, seqs, tokens, HEAD_DIM)

    def attend_back(chip, d_attn, earlier):
        def at(i):
            return 2 * i + chip

        def half_of(first):
            return pl.BlockSpec((first, 1, tokens, HEAD_DIM), lambda i: (0, at(i), 0, 0))

        by_seq_rows = pl.BlockSpec((tokens, group * HEAD_DIM), lambda i: (at(i), 0))
        return attention_call(
            attend_back_kernel,
            both,
            2,
            at,
            [(queries.shape, BF16)] + [(pair, BF16)] * (n_ctx - 1) + [((1, *pair[1:]), BF16)] * 2,
            [queries, *d_attn, output_full, rows_pos[None, :], key_pos[:, None], cosines, sines],
            [by_seq_rows, fixed(tokens, width), fixed(tokens, width)]
            + [fixed(*output_full.shape), fixed(1, group * tokens), fixed(count, 1)]
            + [angles, angles],
            [by_seq_rows] + [half_of(2)] * (n_ctx - 1) + [half_of(1)] * 2,
            earlier,
        )

    d_attn_far, d_attn_near = far_hop(d_attn_own), near_hop(d_attn_own)
    earlier = attend_back(0, [d_attn_own, d_attn_near], ())
    grad_up_part, _ = tie(grad_up_part, d_attn_near)
    grad_up_full = weight_grad(*sides, (2, 1, grad_up_part))
    d_attn_far, earlier, grad_up_full = tie(d_attn_far, earlier, grad_up_full)
    flying["up"] = to_owner(grad_up_full)
    d_attn_last = near_hop(d_attn_far)
    d_query_raw, *d_both = attend_back(1, [d_attn_far, d_attn_last], earlier)
    d_attn = jnp.concatenate([d_attn_own, d_attn_far, d_attn_near, d_attn_last], axis=0)

    def both_of(distance):
        at = max(2 * distance - 1, 0)
        return d_both[at : at + (1 if distance == 0 else 2)]

    def query_work(i, state):
        if i == half_ring - 2:
            return weight_grad(*state[0]), *state[1:]
        if i == half_ring - 3:
            flying["gate"] = to_owner(state[0])
            return weight_grad(*state[1])
        if i == 0:
            flying["down"] = to_owner(state)
            return (
                flying.pop("up"),
                tn(d_query_raw, normed_one).astype(BF16),
                tn(mixed, d_attn).astype(BF16),
            )
        return state

    d_both, state = ring_scatter(
        lambda i, blocks: blocks,
        [both_of(distance) for distance in range(half_ring + 1)],
        query_work,
        ((d_gate, normed_two), (hidden, d_mlp)),
        add_terms_here,
    )
    grad_up, grad_query_full, grad_output_full = state
    d_key_raw, d_value_raw, grad_key_full, grad_value_full = keys_back(
        d_both, cosine, sine, normed_one
    )
    grad_fulls = [grad_query_full, grad_key_full, grad_value_full, grad_output_full]

    ready = {}

    def weight_terms(i, fulls):
        if i == half_ring:
            member = ring_member(i)
            return member_rows([(fulls[:2], cols[:2], member), (fulls[2:], cols[2:], member)], BF16)
        if i in ready:
            return ready[i]
        ends = [0] if i == 0 else [-i, i]
        return member_rows([(fulls, cols, ring_member(k)) for k in ends], BF16)

    def input_side(i, state):
        if i == half_ring - 1:
            ds, up = state
            kept, sent, grad_one = input_terms(
                ds, [query_full, key_full, value_full], all_rows, scales
            )
            return kept, sent, jnp.concatenate([grad_one, grad_two, grad_three, grad_four], axis=0), up
        if i == half_ring - 2:
            kept, sent, sums, up = state
            sums = add_from(sums, "fsdp", low_masks())
            fulls, _ = tie(grad_fulls, kept)
            ready[1], ready[0] = weight_terms(1, fulls), weight_terms(0, fulls)
            return kept, near_hop(sent), sums, up.T.astype(F32), flying.pop("gate"), dict(ready)
        if i == half_ring - 3:
            kept, near, sums, up, gate, _ = state
            total = kept + near.astype(F32)
            arrived = far_hop(total[tokens:].astype(BF16))
            sums = add_from(sums, "ctx", low_masks())
            return total[:tokens] + arrived.astype(F32), sums, up, gate
        if i == 0:
            d_normed_one, sums, up, gate = state
            d_rows_attn, _ = norm_back(rows_in, gain_one, d_normed_one)
            sums = add_from(sums, "ctx", high_masks())
            return d_resid + d_rows_attn, sums, up, gate.T.astype(F32)
        return state

    grad_all, state = ring_scatter(
        weight_terms,
        [grad_fulls] * (half_ring + 1),
        input_side,
        ((d_query_raw, d_key_raw, d_value_raw), grad_up),
    )
    grad_all = grad_all[0].astype(F32) + (grad_all[1].astype(F32) + grad_all[2].astype(F32))
    grad_in, grad_gains, grad_up, grad_gate = state
    grad_down, grad_all = tie(flying.pop("down"), grad_all)
    grad_down = grad_down.astype(F32)
    grad_query, grad_key, grad_value, grad_output = (
        grad_all[a:b] for a, b in zip(cuts, cuts[1:])
    )
    grad_query, grad_key, grad_value = grad_query.T, grad_key.T, grad_value.T
    grad_gains = lax.dynamic_slice_in_dim(grad_gains, own_place, share, axis=1)
    return (
        block_out[None],
        grad_in[None],
        grad_query,
        grad_key,
        grad_value,
        grad_output,
        grad_gate,
        grad_up,
        grad_down,
        grad_gains[0],
        grad_gains[1],
        grad_gains[2],
        grad_gains[3],
    )


def solution(mesh):
    rows = P("fsdp", "ctx", None)
    columns = P(None, ("fsdp", "ctx"))
    units = P(("fsdp", "ctx"), None)
    gain = P(("ctx", "fsdp"))
    weights = (columns, columns, columns, units, columns, columns, units)
    return jax.shard_map(
        body,
        mesh=mesh,
        in_specs=(rows, P()) + weights + (gain,) * 4 + (rows,),
        out_specs=(rows, rows) + weights + (gain,) * 4,
        check_vma=False,
    )
```
